256 devices in a mesh: ctx: 16 (over z, x_hi), patch: 16 (over y, x_lo, core).
Axes of the slice: x: 4 (x_hi: 2, x_lo: 2; x = x_hi * 2 + x_lo), y: 4, z: 8, core: 2. Of those that a mesh axis runs over, the one named last changes fastest.
Arguments:
- grad_out: bfloat16 [3072, 5120], P('ctx', 'patch'), may hold values from -6 to 6
- gate_table: float32 [1000, 5120], P(None, 'patch'), may hold values from 0.1 to 1.9
- timestep: int32 [1], replicated, may hold values from 0 to 999
- out_weight: bfloat16 [5120, 4096], P(None, 'patch'), may hold values from -0.09375 to 0.09375
- queries: bfloat16 [3072, 4096], P('ctx', 'patch'), may hold values from -12 to 12
- keys_main: bfloat16 [3072, 4096], P('ctx', 'patch'), may hold values from -8 to 8
- values: bfloat16 [3072, 4096], P('ctx', 'patch'), may hold values from -6 to 6
- cross_queries: bfloat16 [3072, 4096], P('ctx', 'patch'), may hold values from -12 to 12
- text_keys: bfloat16 [512, 4096], P('ctx', 'patch'), may hold values from -8 to 8
- text_values: bfloat16 [512, 4096], P('ctx', 'patch'), may hold values from -6 to 6
- cross_grad: bfloat16 [3072, 4096], P('ctx', 'patch'), may hold values from -6 to 6
- text_count: int32 [1], replicated, may hold values from 128 to 512
Outputs:
- grad_queries: bfloat16 [3072, 4096], P('ctx', 'patch')
- grad_keys: bfloat16 [3072, 4096], P('ctx', 'patch')
- grad_values: bfloat16 [3072, 4096], P('ctx', 'patch')
- grad_cross: bfloat16 [3072, 4096], P('ctx', 'patch')
- grad_text_keys: bfloat16 [512, 4096], P('ctx', 'patch')
- grad_text_values: bfloat16 [512, 4096], P('ctx', 'patch')
- grad_weight: float32 [5120, 4096], P('ctx', 'patch')
The draws below stay inside these ranges and needn't reach their ends.
All inputs are finite; a program needn't handle non-finite values.
Results may differ from the reference program's by a relative error of at most 0.019.
Values may be sent and summed in bfloat16 or wider, within the bound.
A program may use at most 128 MiB of HBM per device.

```python
import math
import jax
import jax.numpy as jnp
from jax import lax

D = 5120
HD = 128
TEXT = 512
STEPS = 1000
TOK_CTX = 192
HEADS = 32
TOKENS = 3072
N_CTX = 16


def row_scales(key, row_count, lowest, highest):
    return jnp.exp(jax.random.uniform(key, (row_count, 1), jnp.float32, math.log(lowest), math.log(highest)))


def draw_queries(key, part):
    key = jax.random.fold_in(key, 11)
    bulk = jnp.clip(jax.random.normal(key, (TOKENS, HEADS * HD), jnp.float32), -6.0, 6.0)
    return bulk.astype(jnp.bfloat16)


def draw_keys_main(key, part):
    key = jax.random.fold_in(key, 12)
    bulk = jnp.clip(jax.random.normal(key, (TOKENS, HEADS * HD), jnp.float32), -2.6, 2.6)
    bulk = bulk * row_scales(jax.random.fold_in(key, 1), TOKENS, 0.3, 3.0)
    return bulk.astype(jnp.bfloat16)


def draw_cross_queries(key, part):
    key = jax.random.fold_in(key, 13)
    bulk = jnp.clip(jax.random.normal(key, (TOKENS, HEADS * HD), jnp.float32), -6.0, 6.0)
    return bulk.astype(jnp.bfloat16)


def draw_text_keys(key, part):
    key = jax.random.fold_in(key, 14)
    bulk = jnp.clip(jax.random.normal(key, (TEXT, HEADS * HD), jnp.float32), -2.6, 2.6)
    bulk = bulk * row_scales(jax.random.fold_in(key, 1), TEXT, 0.3, 3.0)
    return bulk.astype(jnp.bfloat16)


def block_scale(own_key, extent, shards, low, high):
    def one(axis_at, shards_of):
        heights = jax.random.uniform(jax.random.fold_in(jax.random.fold_in(own_key, 6), axis_at), (shards_of,), jnp.float32, low / len(shards), high / len(shards))
        return jnp.repeat(jnp.exp(heights), extent[axis_at] // shards_of).reshape((-1,) + (1,) * (len(extent) - axis_at - 1))

    level = one(*shards[0])
    for cut in shards[1:]:
        level = level * one(*cut)
    return level


def centred(key, dims, spread, limit, cuts=(), kind=jnp.bfloat16):
    values = jax.random.normal(key, dims, jnp.float32) * spread
    if len(cuts) > 0:
        values = block_scale(key, dims, cuts, -0.22, 0.18) * values
    return jnp.clip(values, min=-limit, max=limit).astype(kind)


def setup_inputs(seed: int = 0) -> dict:
    keys = jax.random.split(jax.random.key(seed), 13)
    return {
        "grad_out": centred(keys[0], (TOKENS, D), 1.0, 6.0, ((0, 16), (1, 16))),
        "gate_table": jnp.clip(1.0 + 0.18 * jax.random.normal(keys[1], (STEPS, D), jnp.float32), 0.1, 1.9),
        "timestep": jax.random.randint(keys[2], (1,), 0, STEPS).astype(jnp.int32),
        "out_weight": centred(keys[3], (D, HEADS * HD), (HEADS * HD) ** -0.5, 0.09375, ((1, 16),)),
        "queries": draw_queries(jax.random.fold_in(keys[12], 71), 0),
        "keys_main": draw_keys_main(jax.random.fold_in(keys[12], 71), 0),
        "values": centred(keys[6], (TOKENS, HEADS * HD), 1.0, 6.0, ((0, 16), (1, 16))),
        "cross_queries": draw_cross_queries(jax.random.fold_in(keys[12], 71), 0),
        "text_keys": draw_text_keys(jax.random.fold_in(keys[12], 71), 0),
        "text_values": centred(keys[9], (TEXT, HEADS * HD), 1.0, 6.0, ((0, 16), (1, 16))),
        "cross_grad": centred(keys[10], (TOKENS, HEADS * HD), 1.0, 6.0, ((0, 16), (1, 16))),
        "text_count": jax.random.randint(keys[11], (1,), TEXT // 4, TEXT + 1).astype(jnp.int32),
    }


def rounded_sum(partials):
    return lax.optimization_barrier(jnp.sum(lax.optimization_barrier(partials.astype(jnp.bfloat16)).astype(jnp.float32), axis=0))

def head_major(matrix):
    return matrix.reshape(matrix.shape[0], HEADS, HD).transpose(1, 0, 2)

def row_major(stacked):
    return stacked.transpose(1, 0, 2).reshape(stacked.shape[1], HEADS * HD)

def attend(query_mat, key_mat, value_mat, grad_mat, live_cols, factor):
    scores = factor * jnp.dot(query_mat, key_mat.T, preferred_element_type=jnp.float32)
    scores = jnp.where(live_cols, scores, -jnp.inf)
    row_top = lax.optimization_barrier(jnp.max(scores, axis=1, keepdims=True))
    log_mass = row_top + jnp.log(lax.optimization_barrier(jnp.sum(jnp.exp(scores - row_top), axis=1, keepdims=True)))
    attn_probs = jnp.exp(scores - log_mass).astype(jnp.bfloat16)
    attn_out = jnp.dot(attn_probs, value_mat, preferred_element_type=jnp.float32)
    row_delta = lax.optimization_barrier(jnp.sum(grad_mat.astype(jnp.float32) * attn_out, axis=1, keepdims=True))
    grad_probs = jnp.dot(grad_mat, value_mat.T, preferred_element_type=jnp.float32)
    grad_scores = (attn_probs.astype(jnp.float32) * (grad_probs - row_delta)).astype(jnp.bfloat16)
    grad_query = (factor * jnp.dot(grad_scores, key_mat, preferred_element_type=jnp.float32)).astype(jnp.bfloat16)
    key_count = key_mat.shape[0]
    score_groups = grad_scores.reshape(N_CTX, TOK_CTX, key_count).astype(jnp.float32)
    prob_groups = attn_probs.reshape(N_CTX, TOK_CTX, key_count).astype(jnp.float32)
    query_groups = query_mat.reshape(N_CTX, TOK_CTX, HD).astype(jnp.float32)
    grad_groups = grad_mat.reshape(N_CTX, TOK_CTX, HD).astype(jnp.float32)
    grad_key = rounded_sum(factor * jnp.einsum('gqk,gqd->gkd', score_groups, query_groups)).astype(jnp.bfloat16)
    grad_value = rounded_sum(jnp.einsum('gqk,gqd->gkd', prob_groups, grad_groups)).astype(jnp.bfloat16)
    return (grad_query, grad_key, grad_value, attn_out)

def reference(grad_out, gate_table, timestep, out_weight, queries, keys_main, values, cross_queries, text_keys, text_values, cross_grad, text_count):
    factor = 1.0 / math.sqrt(HD)
    gate_row = gate_table[timestep[0]]
    scaled = (gate_row[None, :] * grad_out.astype(jnp.float32)).astype(jnp.bfloat16)
    grad_attn = jnp.dot(scaled, out_weight, preferred_element_type=jnp.float32).astype(jnp.bfloat16)
    live_cols = lax.broadcasted_iota(jnp.int32, (1, TEXT), 1) < text_count[0]

    def per_head(operands):
        head_q, head_k, head_v, head_g, head_cq, head_tk, head_tv, head_cg = operands
        self_part = attend(head_q, head_k, head_v, head_g, True, factor)
        cross_part = attend(head_cq, head_tk, head_tv, head_cg, live_cols, factor)
        return self_part + cross_part[:3]
    inputs = (head_major(queries), head_major(keys_main), head_major(values), head_major(grad_attn), head_major(cross_queries), head_major(text_keys), head_major(text_values), head_major(cross_grad))
    results = lax.map(per_head, inputs)
    grad_queries = row_major(results[0])
    grad_keys = row_major(results[1])
    grad_values = row_major(results[2])
    attn_rounded = row_major(results[3]).astype(jnp.bfloat16)
    grad_cross = row_major(results[4])
    grad_text_keys = row_major(results[5])
    grad_text_values = row_major(results[6])
    scaled_groups = scaled.reshape(N_CTX, TOK_CTX, D)
    attn_groups = attn_rounded.reshape(N_CTX, TOK_CTX, HEADS * HD)

    def add_group(running, pair):
        term = jnp.dot(pair[0].T, pair[1], preferred_element_type=jnp.float32)
        return (running + lax.optimization_barrier(term.astype(jnp.bfloat16)).astype(jnp.float32), None)
    grad_weight, _ = lax.scan(add_group, jnp.zeros((D, HEADS * HD), jnp.float32), (scaled_groups, attn_groups))
    return (grad_queries, grad_keys, grad_values, grad_cross, grad_text_keys, grad_text_values, grad_weight)
```

```python
import functools
import math

import jax
import jax.numpy as jnp
from jax import lax
from jax.experimental import pallas as pl
from jax.experimental.pallas import tpu as pltpu
from jax.sharding import PartitionSpec as P

HD = 128
TOK = 192
PAIR = 2 * TOK
TXT = 32
UNIT = 2 * TOK + 2 * TXT
NZ = 8
FEAT = 320
FPAD = 384
D = 5120
BF = jnp.bfloat16
F32 = jnp.float32
MESH = pl.DeviceIdType.MESH
FACTOR = 1.0 / math.sqrt(HD)

NN = (((1,), (0,)), ((), ()))
NT = (((1,), (1,)), ((), ()))
TN = (((0,), (0,)), ((), ()))


def mm(a, b, dims):
    return lax.dot_general(a, b, dims, preferred_element_type=F32)


def kernel(
    go_h, gate_h, ts_s, w_h, q_h, k_h, v_h, cq_h, tk_h, tv_h, cg_h, tc_s,
    gq_o, gk_o, gv_o, gc_o, gtk_o, gtv_o, gw_o,
    U, XS, QA, QS, GO, GT, W, SL, SB, GS, GR, AT, ST, STAT, OT, DQT, DO, R, RR, GP, GG, FR, DQ, DR,
    OQ, OK, OV, OC, OTK, OTV, OW,
    ld, st, xs, xr, ags, agr, s1s, s1r, s2s, s2r, s3s, s3r, ks, kr, gs, gr,
):
    c = lax.axis_index("ctx")
    p = lax.axis_index("patch")
    z, xh = c // 2, lax.rem(c, 2)
    ox = 1 - xh
    y, core, xlo = p // 4, lax.rem(p, 2), lax.rem(p // 2, 2)
    zr = lambda n: lax.rem(z + n + NZ, NZ)
    partner = (2 * z + ox, p)
    right = (2 * zr(1) + xh, p)
    left = (2 * zr(-1) + xh, p)
    ydev = [(c, lax.rem(y + n, 4) * 4 + xlo * 2 + core) for n in (1, 2, 3)]
    sibling = (c, p + 1 - 2 * core)
    s1_same = (2 * z + core, y * 4 + xlo * 2 + xh)
    s1_flip = (2 * z + core, y * 4 + (1 - xlo) * 2 + xh)
    is_self = core == xh
    own_cols = pl.ds(pl.multiple_of(xh * HD, HD), HD)
    other_cols = pl.ds(pl.multiple_of(ox * HD, HD), HD)

    def remote(src, dst, send, recv, dev):
        return pltpu.make_async_remote_copy(
            src_ref=src, dst_ref=dst, send_sem=send, recv_sem=recv, device_id=dev, device_id_type=MESH
        )

    pending = []

    def push(src, dst, send, recv, dev):
        copy = remote(src, dst, send, recv, dev)
        copy.start()
        pending.append(copy)

    def arrive(dst, send, recv):
        remote(dst, dst, send, recv, partner).wait_recv()

    loads = []

    def load(src, dst):
        copy = pltpu.make_async_copy(src, dst, ld.at[len(loads)])
        copy.start()
        loads.append(copy)

    for src, at, rows in ((k_h, 0, TOK), (v_h, TOK, TOK), (tk_h, PAIR, TXT), (tv_h, PAIR + TXT, TXT)):
        load(src.at[:, other_cols], XS.at[pl.ds(at, rows)])
        load(src.at[:, own_cols], U.at[c, pl.ds(at, rows)])
    load(go_h, GO)
    load(gate_h, GT)
    for n, src in enumerate((q_h, cq_h, cg_h)):
        load(src.at[:, other_cols], QS.at[n])
        load(src.at[:, own_cols], QA.at[n, xh])
    load(w_h, W.at[pl.ds(0, D)])
    W[pl.ds(D, FPAD - FEAT), :] = jnp.zeros((FPAD - FEAT, 2 * HD), BF)

    barrier = pltpu.get_barrier_semaphore()
    diagonal = (2 * z + ox, sibling[1])
    for dev in [partner, right, left, sibling, s1_flip, diagonal] + ydev:
        pl.semaphore_signal(barrier, inc=1, device_id=dev, device_id_type=MESH)
    pl.semaphore_wait(barrier, 9)

    for n in range(8):
        loads[n].wait()

    push(XS, U.at[c], xs.at[0], xr.at[0], partner)

    def ag_send(stream, side, n):
        unit = 2 * (zr(-n) if side == 0 else zr(n)) + (xh if stream == 0 else ox)
        push(U.at[unit], U.at[unit], ags.at[stream, side, n], agr.at[stream, side, n], right if side == 0 else left)

    def ag_recv(stream, side, n):
        unit = 2 * (zr(-n - 1) if side == 0 else zr(n + 1)) + (xh if stream == 0 else ox)
        arrive(U.at[unit], ags.at[stream, side, n], agr.at[stream, side, n])

    def ag_len(stream, side):
        return 4 if stream == side else 3

    ag_send(0, 0, 0)
    ag_send(0, 1, 0)

    loads[8].wait()
    loads[9].wait()
    gate_row = GT[pl.ds(ts_s[0], 1), :]
    scaled = (gate_row * GO[...].astype(F32)).astype(BF)
    SL[...] = jnp.concatenate([scaled, jnp.zeros((TOK, FPAD - FEAT), BF)], axis=1)
    j0 = 2 * y + xlo
    push(SL, SB.at[xh, j0], s1s.at[1], s1r.at[xlo], s1_flip)

    @pl.when(is_self)
    def _():
        SB[xh, j0] = SL[...]

    @pl.when(jnp.logical_not(is_self))
    def _():
        remote(SL, SB.at[xh, j0], s1s.at[0], s1r.at[xlo], s1_same).start()

    for n in range(10, 16):
        loads[n].wait()
    push(QS, QA.at[:, xh], xs.at[1], xr.at[1], partner)

    arrive(U.at[2 * z + ox], xs.at[0], xr.at[0])
    ag_send(1, 0, 0)
    ag_send(1, 1, 0)

    arrive(SB.at[core, 2 * y + 1 - xlo], s1s.at[1], s1r.at[1 - xlo])

    @pl.when(jnp.logical_not(is_self))
    def _():
        arrive(SB.at[core, 2 * y + xlo], s1s.at[0], s1r.at[xlo])

    pair_at = lambda yy: SB.at[core, pl.ds(2 * yy, 2)]
    for n in range(3):
        push(pair_at(y), pair_at(y), s2s.at[n], s2r.at[n], ydev[n])
    push(pair_at(y), pair_at(y), s3s.at[0], s3r.at[0], sibling)

    arrive(QA.at[:, ox], xs.at[1], xr.at[1])

    STAT[...] = jnp.full((8, PAIR), -jnp.inf, F32)
    STAT[pl.ds(1, 1), :] = jnp.zeros((1, PAIR), F32)
    OT[...] = jnp.zeros((HD, PAIR), F32)
    DQT[...] = jnp.zeros((HD, PAIR), F32)

    def stacked(index):
        return QA[index].reshape(PAIR, HD)

    def rows_of(zb, at, rows):
        return jnp.concatenate([U[2 * zb, at : at + rows], U[2 * zb + 1, at : at + rows]], axis=0)

    def forward(zb):
        scores = FACTOR * mm(rows_of(zb, 0, TOK), stacked(0), NT)
        ST[zb] = scores
        top = STAT[0:1]
        new_top = jnp.maximum(top, jnp.max(scores, axis=0, keepdims=True))
        decay = jnp.exp(top - new_top)
        probs = jnp.exp(scores - new_top)
        STAT[0:1] = new_top
        STAT[1:2] = STAT[1:2] * decay + jnp.sum(probs, axis=0, keepdims=True)
        OT[...] = OT[...] * decay + mm(rows_of(zb, TOK, TOK), probs.astype(BF), TN)

    def forward_sides(n):
        def one(side, carry):
            forward(zr((2 * side - 1) * n))
            return carry

        lax.fori_loop(0, 2, one, 0)

    forward(z)
    for n in range(4):
        for stream, side in ((0, 0), (0, 1), (1, 0), (1, 1)):
            length = ag_len(stream, side)
            if n < length:
                ag_recv(stream, side, n)
                if n + 1 < length:
                    ag_send(stream, side, n + 1)
        if n == 0:
            forward_sides(1)
            for m in range(3):
                frm = lax.rem(y + 3 - m, 4)
                arrive(pair_at(frm), s2s.at[m], s2r.at[m])
                push(pair_at(frm), pair_at(frm), s3s.at[m + 1], s3r.at[m + 1], sibling)
        elif n == 1:
            forward_sides(2)
            for m in range(4):
                frm = lax.rem(y + 4 - m, 4)
                arrive(SB.at[1 - core, pl.ds(2 * frm, 2)], s3s.at[m], s3r.at[m])
            loads[16].wait()

            def part(j, total):
                rows = jnp.concatenate([SB[0, j], SB[1, j]], axis=0)
                weight = W[pl.ds(pl.multiple_of(FEAT * (2 * j + xh), 64), FPAD), :]
                return total + mm(rows, weight, NN)

            total = lax.fori_loop(0, NZ, part, jnp.zeros((PAIR, 2 * HD), F32))
            low, high = total[:, :HD], total[:, HD:]
            mine = xh == 0
            GS[...] = jnp.where(mine, high, low).astype(BF)
            push(GS, GR, xs.at[2], xr.at[2], partner)
            DO[...] = jnp.where(mine, low, high)
        elif n == 2:
            forward_sides(3)
            arrive(GR, xs.at[2], xr.at[2])
            DO[...] = DO[...] + GR[...].astype(F32)
        else:
            forward(zr(4))

    mass = STAT[1:2]
    log_mass = STAT[0:1] + jnp.log(mass)
    attn = OT[...] / mass
    AT[xh] = attn.astype(BF)
    push(AT.at[xh], AT.at[xh], xs.at[3], xr.at[3], partner)
    STAT[2:3] = log_mass
    grad = DO[...]
    grad = grad.astype(BF)
    STAT[3:4] = jnp.sum(grad.astype(F32).T * attn, axis=0, keepdims=True)

    def text_rows(at):
        return U[:, at : at + TXT, :].reshape(2 * NZ * TXT, HD)

    tkeys, tvalues, cgrad, cquery = text_rows(PAIR), text_rows(PAIR + TXT), stacked(2), stacked(1)
    tscores = FACTOR * mm(tkeys, cquery, NT)
    live = lax.broadcasted_iota(jnp.int32, (2 * NZ * TXT, 1), 0) < tc_s[0]
    tscores = jnp.where(live, tscores, -jnp.inf)
    ttop = jnp.max(tscores, axis=0, keepdims=True)
    tmass = ttop + jnp.log(jnp.sum(jnp.exp(tscores - ttop), axis=0, keepdims=True))
    tprobs = jnp.exp(tscores - tmass).astype(BF)
    tgrad_probs = mm(tvalues, cgrad, NT)
    tdelta = jnp.sum(cgrad.astype(F32).T * mm(tvalues, tprobs, TN), axis=0, keepdims=True)
    tgrad_scores = (tprobs.astype(F32) * (tgrad_probs - tdelta)).astype(BF)
    dcross = FACTOR * mm(tkeys, tgrad_scores, TN)
    DQ[1] = dcross.T.astype(BF).reshape(2, TOK, HD)
    R[:, PAIR : PAIR + TXT, :] = (FACTOR * mm(tgrad_scores, cquery, NN)).astype(BF).reshape(2 * NZ, TXT, HD)
    R[:, PAIR + TXT : UNIT, :] = mm(tprobs, cgrad, NN).astype(BF).reshape(2 * NZ, TXT, HD)
    DO[...] = grad.astype(F32)

    def backward(zb):
        keys, vals = rows_of(zb, 0, TOK), rows_of(zb, TOK, TOK)
        out_grad = DO[...].astype(BF)
        probs = jnp.exp(ST[zb] - STAT[2:3]).astype(BF)
        grad_scores = (probs.astype(F32) * (mm(vals, out_grad, NT) - STAT[3:4])).astype(BF)
        dvals = mm(probs, out_grad, NN).astype(BF)
        dkeys = (FACTOR * mm(grad_scores, stacked(0), NN)).astype(BF)
        DQT[...] = DQT[...] + mm(keys, grad_scores, TN)
        for s in range(2):
            R[2 * zb + s, 0:TOK] = dkeys[s * TOK : (s + 1) * TOK]
            R[2 * zb + s, TOK:PAIR] = dvals[s * TOK : (s + 1) * TOK]

    def weight_part(j):
        rows = jnp.concatenate([SB[0, j], SB[1, j]], axis=0)
        part = mm(AT[...].reshape(2 * HD, PAIR), rows, NN).astype(BF)
        for h in range(2):
            for b in range(2):
                GP[j, (2 * h + b) * HD : (2 * h + b + 1) * HD] = part[h * HD : (h + 1) * HD, b * HD : (b + 1) * HD]
        GP[j, 4 * HD : 5 * HD] = jnp.concatenate([part[:HD, 2 * HD : FEAT], part[HD:, 2 * HD : FEAT]], axis=1)

    def sides(n, step):
        if n in (0, 4):
            step(zr(n))
        else:

            def one(side, carry):
                step(zr((1 - 2 * side) * n))
                return carry

            lax.fori_loop(0, 2, one, 0)

    def rs_len(side, unit):
        return 4 if side == unit else 3

    def add_kv(index, slot):
        R[index] = (R[index].astype(F32) + slot[...].astype(F32)).astype(BF)

    def half(unit):
        return pl.ds(unit * FEAT, FEAT)

    for n in (4, 3, 2, 1, 0):
        sides(n, backward)
        for side in range(2):
            dest = zr(n) if side == 0 else zr(-n)
            dev = right if side == 0 else left
            for unit in range(2):
                length = rs_len(side, unit)
                if n < length:
                    arrive(RR.at[side, unit, n], ks.at[side, unit, n], kr.at[side, unit, n])
                    add_kv(2 * dest + unit, RR.at[side, unit, n])
                if 0 < n <= length:
                    push(R.at[2 * dest + unit], RR.at[side, unit, n - 1], ks.at[side, unit, n - 1], kr.at[side, unit, n - 1], dev)
        if n == 4:
            arrive(AT.at[ox], xs.at[3], xr.at[3])
        if n == 0:
            push(R.at[2 * z + ox], FR, xs.at[4], xr.at[4], partner)
            DQ[0] = (FACTOR * DQT[...]).T.astype(BF).reshape(2, TOK, HD)
            push(DQ.at[:, ox], DR, xs.at[5], xr.at[5], partner)
        sides(n, weight_part)
        for side in range(2):
            dest = zr(n) if side == 0 else zr(-n)
            dev = right if side == 0 else left
            for unit in range(2):
                length = rs_len(side, unit)
                if n < length:
                    arrive(GG.at[side, unit, n], gs.at[side, unit, n], gr.at[side, unit, n])
                    if n > 0:
                        GP[dest, half(unit)] = (
                            GP[dest, half(unit)].astype(F32) + GG[side, unit, n].astype(F32)
                        ).astype(BF)
                if 0 < n <= length:
                    push(GP.at[dest, half(unit)], GG.at[side, unit, n - 1], gs.at[side, unit, n - 1], gr.at[side, unit, n - 1], dev)

    stores = []

    def store(src, dst):
        copy = pltpu.make_async_copy(src, dst, st.at[len(stores)])
        copy.start()
        stores.append(copy)

    total = jnp.concatenate(
        [
            GP[z, half(unit)].astype(F32) + GG[0, unit, 0].astype(F32) + GG[1, unit, 0].astype(F32)
            for unit in range(2)
        ],
        axis=0,
    )
    for h in range(2):
        for b in range(2):
            at = (2 * h + b) * HD
            OW[b * HD : (b + 1) * HD, h * HD : (h + 1) * HD] = total[at : at + HD].T
    last = total[4 * HD :].T
    for h in range(2):
        OW[2 * HD : FEAT, h * HD : (h + 1) * HD] = last[h * 64 : (h + 1) * 64]
    store(OW, gw_o)

    arrive(FR, xs.at[4], xr.at[4])
    arrive(DR, xs.at[5], xr.at[5])
    for ref, out, at, rows in ((OK, gk_o, 0, TOK), (OV, gv_o, TOK, TOK), (OTK, gtk_o, PAIR, TXT), (OTV, gtv_o, PAIR + TXT, TXT)):
        ref[:, own_cols] = R[c, at : at + rows]
        ref[:, other_cols] = FR[at : at + rows]
        store(ref, out)
    for n, (ref, out) in enumerate(((OQ, gq_o), (OC, gc_o))):
        ref[:, own_cols] = DQ[n, xh]
        ref[:, other_cols] = DR[n]
        store(ref, out)
    for copy in pending:
        copy.wait_send()

    @pl.when(jnp.logical_not(is_self))
    def _():
        remote(SL, SB.at[xh, j0], s1s.at[0], s1r.at[xlo], s1_same).wait_send()

    for copy in stores:
        copy.wait()


def local(*args):
    any_spec = pl.BlockSpec(memory_space=pl.ANY)
    smem = pl.BlockSpec(memory_space=pltpu.SMEM)
    in_specs = [any_spec] * 12
    in_specs[2] = in_specs[11] = smem
    outs = [
        jax.ShapeDtypeStruct((TOK, 2 * HD), BF),
        jax.ShapeDtypeStruct((TOK, 2 * HD), BF),
        jax.ShapeDtypeStruct((TOK, 2 * HD), BF),
        jax.ShapeDtypeStruct((TOK, 2 * HD), BF),
        jax.ShapeDtypeStruct((TXT, 2 * HD), BF),
        jax.ShapeDtypeStruct((TXT, 2 * HD), BF),
        jax.ShapeDtypeStruct((FEAT, 2 * HD), F32),
    ]
    V = pltpu.VMEM
    S = pltpu.SemaphoreType.DMA
    scratch = [
        V((2 * NZ, UNIT, HD), BF),
        V((UNIT, HD), BF),
        V((3, 2, TOK, HD), BF),
        V((3, TOK, HD), BF),
        V((TOK, FEAT), BF),
        V((1000, FEAT), F32),
        V((D + FPAD - FEAT, 2 * HD), BF),
        V((TOK, FPAD), BF),
        V((2, NZ, TOK, FPAD), BF),
        V((PAIR, HD), BF),
        V((PAIR, HD), BF),
        V((2, HD, PAIR), BF),
        V((NZ, PAIR, PAIR), F32),
        V((8, PAIR), F32),
        V((HD, PAIR), F32),
        V((HD, PAIR), F32),
        V((PAIR, HD), F32),
        V((2 * NZ, UNIT, HD), BF),
        V((2, 2, 4, UNIT, HD), BF),
        V((NZ, 2 * FEAT, HD), BF),
        V((2, 2, 4, FEAT, HD), BF),
        V((UNIT, HD), BF),
        V((2, 2, TOK, HD), BF),
        V((2, TOK, HD), BF),
        V((TOK, 2 * HD), BF),
        V((TOK, 2 * HD), BF),
        V((TOK, 2 * HD), BF),
        V((TOK, 2 * HD), BF),
        V((TXT, 2 * HD), BF),
        V((TXT, 2 * HD), BF),
        V((FEAT, 2 * HD), F32),
        S((17,)),
        S((7,)),
        S((6,)),
        S((6,)),
        S((2, 2, 4)),
        S((2, 2, 4)),
        S((2,)),
        S((2,)),
        S((3,)),
        S((3,)),
        S((4,)),
        S((4,)),
        S((2, 2, 4)),
        S((2, 2, 4)),
        S((2, 2, 4)),
        S((2, 2, 4)),
    ]
    return pl.pallas_call(
        kernel,
        out_shape=outs,
        in_specs=in_specs,
        out_specs=[any_spec] * 7,
        scratch_shapes=scratch,
        compiler_params=pltpu.CompilerParams(
            collective_id=0, has_side_effects=True, vmem_limit_bytes=56 * 1024 * 1024
        ),
    )(*args)


def solution(mesh):
    return jax.shard_map(
        local,
        mesh=mesh,
        in_specs=(
            P("ctx", "patch"),
            P(None, "patch"),
            P(),
            P(None, "patch"),
            P("ctx", "patch"),
            P("ctx", "patch"),
            P("ctx", "patch"),
            P("ctx", "patch"),
            P("ctx", "patch"),
            P("ctx", "patch"),
            P("ctx", "patch"),
            P(),
        ),
        out_specs=(P("ctx", "patch"),) * 7,
        check_vma=False,
    )
```

```python
import math

import jax
import jax.numpy as jnp
from jax import lax
from jax.experimental import pallas as pl
from jax.experimental.pallas import tpu as pltpu
from jax.sharding import PartitionSpec as P

HD = 128
TOK = 192
PAIR = 2 * TOK
TXT = 32
NZ = 8
FEAT = 320
FPAD = 384
PACK = 2 * TOK + TOK // 2
D = 5120
STEPS = 1000
BF = jnp.bfloat16
F32 = jnp.float32
MESH = pl.DeviceIdType.MESH
FACTOR = 1.0 / math.sqrt(HD)

NN = (((1,), (0,)), ((), ()))
NT = (((1,), (1,)), ((), ()))
TN = (((0,), (0,)), ((), ()))


def mm(a, b, dims):
    return lax.dot_general(a, b, dims, preferred_element_type=F32)


def kernel(
    go_h, gate_h, ts_s, w_h, q_h, k_h, v_h, cq_h, tk_h, tv_h, cg_h, tc_s,
    gq_o, gk_o, gv_o, gc_o, gtk_o, gtv_o, gw_o,
    U, UT, XT, XK, QA, QS, GO, GT, W, SL, SB, SU, GS, GR, AT, ST, STAT, OT, DQT, DO, DW, DOB, R, RT, RR, RRT, GP, GG, FR, FRT, DQ, DR,
    OQ, OK, OV, OC, OTK, OTV, OW,
    ld, st, xs, xr, ags, agr, ats, atr, s1s, s1r, s2s, s2r, s2fs, s2fr, s3s, s3r, ks, kr, ts, tr, gs, gr,
):
    c = lax.axis_index("ctx")
    p = lax.axis_index("patch")
    z, xh = c // 2, lax.rem(c, 2)
    ox = 1 - xh
    y, core, xlo = p // 4, lax.rem(p, 2), lax.rem(p // 2, 2)
    zr = lambda n: lax.rem(z + n + NZ, NZ)
    yr = lambda n: lax.rem(y + n + 4, 4)
    partner = (2 * z + ox, p)
    right = (2 * zr(1) + xh, p)
    left = (2 * zr(-1) + xh, p)
    ydev = [(c, yr(n) * 4 + xlo * 2 + core) for n in (1, -1)]
    sibling = (c, p + 1 - 2 * core)
    s1_same = (2 * z + core, y * 4 + xlo * 2 + xh)
    s1_flip = (2 * z + core, y * 4 + (1 - xlo) * 2 + xh)
    diagonal = (2 * z + ox, sibling[1])
    is_self = core == xh
    own_cols = pl.ds(pl.multiple_of(xh * HD, HD), HD)
    other_cols = pl.ds(pl.multiple_of(ox * HD, HD), HD)

    def remote(src, dst, send, recv, dev):
        return pltpu.make_async_remote_copy(
            src_ref=src, dst_ref=dst, send_sem=send, recv_sem=recv, device_id=dev, device_id_type=MESH
        )

    pending = []

    def push(src, dst, send, recv, dev):
        copy = remote(src, dst, send, recv, dev)
        copy.start()
        pending.append(copy)

    def arrive(dst, send, recv):
        remote(dst, dst, send, recv, partner).wait_recv()

    loads = []

    def load(src, dst):
        copy = pltpu.make_async_copy(src, dst, ld.at[len(loads)])
        copy.start()
        loads.append(copy)

    load(gate_h, GT)
    load(go_h, GO)
    load(tk_h.at[:, own_cols], UT.at[c, pl.ds(0, TXT)])
    load(tv_h.at[:, own_cols], UT.at[c, pl.ds(TXT, TXT)])
    load(k_h.at[:, own_cols], U.at[c, pl.ds(0, TOK)])
    load(v_h.at[:, own_cols], U.at[c, pl.ds(TOK, TOK)])
    for n, src in enumerate((q_h, cq_h, cg_h)):
        load(src.at[:, own_cols], QA.at[n, xh])
    load(w_h, W.at[pl.ds(0, D)])
    load(tk_h.at[:, other_cols], XT.at[pl.ds(0, TXT)])
    load(tv_h.at[:, other_cols], XT.at[pl.ds(TXT, TXT)])
    load(k_h.at[:, other_cols], XK.at[pl.ds(0, TOK)])
    load(v_h.at[:, other_cols], XK.at[pl.ds(TOK, TOK)])
    for n, src in enumerate((q_h, cq_h, cg_h)):
        load(src.at[:, other_cols], QS.at[n])

    barrier = pltpu.get_barrier_semaphore()
    for dev in [partner, right, left, sibling, s1_flip, diagonal] + ydev:
        pl.semaphore_signal(barrier, inc=1, device_id=dev, device_id_type=MESH)
    W[pl.ds(D, FPAD - FEAT), :] = jnp.zeros((FPAD - FEAT, 2 * HD), BF)
    STAT[...] = jnp.full((8, PAIR), -jnp.inf, F32)
    STAT[1:2, :] = jnp.zeros((1, PAIR), F32)
    OT[...] = jnp.zeros((HD, PAIR), F32)
    DQT[...] = jnp.zeros((HD, PAIR), F32)
    DW[...] = jnp.zeros((PAIR, 2 * HD), F32)
    pl.semaphore_wait(barrier, 8)

    def cross_x(n, src, dst, *waits):
        for at in waits:
            loads[at].wait()
        push(src, dst, xs.at[n], xr.at[n], partner)

    cross_x(0, XT, UT.at[c], 10, 11)
    cross_x(2, XK, U.at[c], 12, 13)

    def ag_len(stream, side):
        return 4 if stream == side else 3

    def ag_unit(stream, side, n):
        return 2 * (zr(-n) if side == 0 else zr(n)) + (xh if stream == 0 else ox)

    def ag_send(buf, ss, rs, stream, side, n):
        if n < ag_len(stream, side):
            unit = ag_unit(stream, side, n)
            at = (stream, side, n)
            push(buf.at[unit], buf.at[unit], ss.at[at], rs.at[at], right if side == 0 else left)

    def ag_step(buf, ss, rs, stream, n):
        units = []
        for side in range(2):
            if n < ag_len(stream, side):
                unit = ag_unit(stream, side, n + 1)
                arrive(buf.at[unit], ss.at[stream, side, n], rs.at[stream, side, n])
                ag_send(buf, ss, rs, stream, side, n + 1)
                units.append(unit)
        return units

    def text_step(n):
        for stream in range(2):
            ag_step(UT, ats, atr, stream, n)

    loads[2].wait()
    loads[3].wait()
    for side in range(2):
        ag_send(UT, ats, atr, 0, side, 0)
    loads[4].wait()
    loads[5].wait()
    for side in range(2):
        ag_send(U, ags, agr, 0, side, 0)

    loads[0].wait()
    loads[1].wait()
    chosen = lax.broadcasted_iota(jnp.int32, (1, STEPS), 1) == ts_s[0]
    gate_col = jnp.sum(jnp.where(chosen, GT[...], 0.0), axis=1, keepdims=True)
    gate_row = jnp.broadcast_to(gate_col, (FEAT, HD)).T[0:1]
    scaled = (gate_row * GO[...].astype(F32)).astype(BF)
    SL[0:TOK] = scaled[:, :HD]
    SL[TOK:PAIR] = scaled[:, HD : 2 * HD]
    SL[PAIR:PACK] = jnp.concatenate([scaled[: TOK // 2, 2 * HD :], scaled[TOK // 2 :, 2 * HD :]], axis=1)
    j0 = 2 * y + xlo
    push(SL, SB.at[xh, j0], s1s.at[1], s1r.at[xlo], s1_flip)

    @pl.when(is_self)
    def _():
        SB[xh, j0] = SL[...]

    @pl.when(jnp.logical_not(is_self))
    def _():
        remote(SL, SB.at[xh, j0], s1s.at[0], s1r.at[xlo], s1_same).start()

    arrive(UT.at[2 * z + ox], xs.at[0], xr.at[0])
    for side in range(2):
        ag_send(UT, ats, atr, 1, side, 0)
    arrive(U.at[2 * z + ox], xs.at[2], xr.at[2])
    for side in range(2):
        ag_send(U, ags, agr, 1, side, 0)

    block = lambda n, b: SB.at[core, 2 * yr(n) + b]

    def own_block(b):
        for n in range(2):
            push(block(0, b), block(0, b), s2s.at[n, b], s2r.at[n, b], ydev[n])
        push(block(0, b), block(0, b), s3s.at[0, b], s3r.at[0, b], sibling)

    def scaled_own():
        @pl.when(jnp.logical_not(is_self))
        def _():
            arrive(block(0, xlo), s1s.at[0], s1r.at[xlo])

        own_block(xlo)
        arrive(block(0, 1 - xlo), s1s.at[1], s1r.at[1 - xlo])
        own_block(1 - xlo)

    def scaled_near():
        for n in range(2):
            frm = 2 * n - 1
            for b in range(2):
                arrive(block(frm, b), s2s.at[n, b], s2r.at[n, b])
                if b == n:
                    push(block(frm, b), block(frm, b), s2fs.at[n], s2fr.at[n], ydev[n])
                push(block(frm, b), block(frm, b), s3s.at[1 + n, b], s3r.at[1 + n, b], sibling)

    def scaled_far():
        for b in range(2):
            arrive(block(2, b), s2fs.at[b], s2fr.at[b])
            push(block(2, b), block(2, b), s3s.at[3, b], s3r.at[3, b], sibling)

    def stacked(index):
        return QA[index].reshape(PAIR, HD)

    def rows_of(zb, at):
        return jnp.concatenate([U[2 * zb, at : at + TOK], U[2 * zb + 1, at : at + TOK]], axis=0)

    def forward(unit):
        scores = FACTOR * mm(U[unit, 0:TOK], stacked(0), NT)
        ST[unit] = scores
        top = STAT[0:1]
        new_top = jnp.maximum(top, jnp.max(scores, axis=0, keepdims=True))
        decay = jnp.exp(top - new_top)
        probs = jnp.exp(scores - new_top)
        STAT[0:1] = new_top
        STAT[1:2] = STAT[1:2] * decay + jnp.sum(probs, axis=0, keepdims=True)
        OT[...] = OT[...] * decay + mm(U[unit, TOK:PAIR], probs.astype(BF), TN)

    def kv_step(stream, n):
        return ag_step(U, ags, agr, stream, n)

    def forward_all(units):
        for unit in units:
            forward(unit)

    def rs_len(side, unit):
        return 4 if side == unit else 3

    def rs_step(n, cur, slots, ss, rs):
        for side in range(2):
            dest = zr(n) if side == 0 else zr(-n)
            dev = right if side == 0 else left
            for unit in range(2):
                length = rs_len(side, unit)
                ref = cur(dest, unit)
                if n < length:
                    slot = slots.at[side, unit, n]
                    arrive(slot, ss.at[side, unit, n], rs.at[side, unit, n])
                    ref[...] = (ref[...].astype(F32) + slot[...].astype(F32)).astype(BF)
                if 0 < n <= length:
                    push(ref, slots.at[side, unit, n - 1], ss.at[side, unit, n - 1], rs.at[side, unit, n - 1], dev)

    def rs_text(n):
        rs_step(n, lambda dest, unit: RT.at[2 * dest + unit], RRT, ts, tr)

    def rs_kv(n):
        rs_step(n, lambda dest, unit: R.at[2 * dest + unit], RR, ks, kr)

    def rs_weight(n):
        rs_step(n, lambda dest, unit: GP.at[dest, pl.ds(unit * FEAT, FEAT)], GG, gs, gr)

    def text():
        tkeys = UT[:, 0:TXT, :].reshape(2 * NZ * TXT, HD)
        tvalues = UT[:, TXT:, :].reshape(2 * NZ * TXT, HD)
        cgrad, cquery = stacked(2), stacked(1)
        tscores = FACTOR * mm(tkeys, cquery, NT)
        live = lax.broadcasted_iota(jnp.int32, (2 * NZ * TXT, 1), 0) < tc_s[0]
        tscores = jnp.where(live, tscores, -jnp.inf)
        ttop = jnp.max(tscores, axis=0, keepdims=True)
        tmass = ttop + jnp.log(jnp.sum(jnp.exp(tscores - ttop), axis=0, keepdims=True))
        tprobs = jnp.exp(tscores - tmass).astype(BF)
        tgrad_probs = mm(tvalues, cgrad, NT)
        tdelta = jnp.sum(cgrad.astype(F32).T * mm(tvalues, tprobs, TN), axis=0, keepdims=True)
        tgrad_scores = (tprobs.astype(F32) * (tgrad_probs - tdelta)).astype(BF)
        RT[:, 0:TXT, :] = (FACTOR * mm(tgrad_scores, cquery, NN)).astype(BF).reshape(2 * NZ, TXT, HD)
        RT[:, TXT:, :] = mm(tprobs, cgrad, NN).astype(BF).reshape(2 * NZ, TXT, HD)
        dcross = FACTOR * mm(tkeys, tgrad_scores, TN)
        DQ[1] = dcross.T.astype(BF).reshape(2, TOK, HD)

    def project_part(frm, n):
        for b in range(2):
            arrive(SB.at[1 - core, 2 * yr(frm) + b], s3s.at[n, b], s3r.at[n, b])

        def part(b, carry):
            j = 2 * yr(frm) + b
            rows = []
            for s in range(2):
                rest = SB[s, j, PAIR:PACK]
                rest = jnp.concatenate([rest[:, : HD // 2], rest[:, HD // 2 :]], axis=0)
                rows.append(
                    jnp.concatenate([SB[s, j, 0:TOK], SB[s, j, TOK:PAIR], rest, jnp.zeros((TOK, HD // 2), BF)], axis=1)
                )
            rows = jnp.concatenate(rows, axis=0)
            SU[j] = rows
            weight = W[pl.ds(pl.multiple_of(FEAT * (2 * j + xh), 64), FPAD), :]
            DW[...] = DW[...] + mm(rows, weight, NN)
            return carry

        lax.fori_loop(0, 2, part, 0)

    def project_end():
        low, high = DW[:, :HD], DW[:, HD:]
        mine = xh == 0
        GS[...] = jnp.where(mine, high, low).astype(BF)
        push(GS, GR, xs.at[7], xr.at[7], partner)
        DO[...] = jnp.where(mine, low, high)

    def backward(zb):
        keys, vals = rows_of(zb, 0), rows_of(zb, TOK)
        out_grad = DOB[...]
        scores = ST[pl.ds(2 * zb, 2)].reshape(PAIR, PAIR)
        probs = jnp.exp(scores - STAT[2:3]).astype(BF)
        grad_scores = (probs.astype(F32) * (mm(vals, out_grad, NT) - STAT[3:4])).astype(BF)
        dvals = mm(probs, out_grad, NN).astype(BF)
        dkeys = (FACTOR * mm(grad_scores, stacked(0), NN)).astype(BF)
        DQT[...] = DQT[...] + mm(keys, grad_scores, TN)
        for s in range(2):
            R[2 * zb + s, 0:TOK] = dkeys[s * TOK : (s + 1) * TOK]
            R[2 * zb + s, TOK:PAIR] = dvals[s * TOK : (s + 1) * TOK]

    def weight_part(j):
        part = mm(AT[...].reshape(2 * HD, PAIR), SU[j], NN).astype(BF)
        for h in range(2):
            for b in range(2):
                GP[j, (2 * h + b) * HD : (2 * h + b + 1) * HD] = part[h * HD : (h + 1) * HD, b * HD : (b + 1) * HD]
        GP[j, 4 * HD : 5 * HD] = jnp.concatenate([part[:HD, 2 * HD : FEAT], part[HD:, 2 * HD : FEAT]], axis=1)

    def sides(n, step):
        if n in (0, 4):
            step(zr(n))
        else:

            def one(side, carry):
                step(zr((1 - 2 * side) * n))
                return carry

            lax.fori_loop(0, 2, one, 0)

    units = kv_step(0, 0)
    text_step(0)
    scaled_own()
    for n in range(3):
        cross_x(4 + n, QS.at[n], QA.at[n, xh], 14 + n)
    more = kv_step(1, 0)
    text_step(1)
    loads[6].wait()
    arrive(QA.at[0, ox], xs.at[4], xr.at[4])
    forward_all([c, 2 * z + ox] + units)
    units = kv_step(0, 1)
    text_step(2)
    forward_all(more)
    scaled_near()
    more = kv_step(1, 1)
    text_step(3)
    loads[9].wait()
    project_part(0, 0)
    forward_all(units + more)
    units = kv_step(0, 2)
    project_part(-1, 1)
    project_part(1, 2)
    scaled_far()
    forward_all(units)
    units = kv_step(1, 2)
    project_part(2, 3)
    project_end()
    loads[7].wait()
    loads[8].wait()
    arrive(QA.at[1, ox], xs.at[5], xr.at[5])
    arrive(QA.at[2, ox], xs.at[6], xr.at[6])
    text()
    rs_text(4)
    forward_all(units)
    units = kv_step(0, 3)
    forward_all(units)
    units = kv_step(1, 3)
    forward_all(units)
    arrive(GR, xs.at[7], xr.at[7])
    DO[...] = DO[...] + GR[...].astype(F32)
    DOB[...] = DO[...].astype(BF)

    mass = STAT[1:2]
    attn = OT[...] / mass
    STAT[2:3] = STAT[0:1] + jnp.log(mass)
    AT[xh] = attn.astype(BF)
    push(AT.at[xh], AT.at[xh], xs.at[8], xr.at[8], partner)
    STAT[3:4] = jnp.sum(DOB[...].astype(F32).T * attn, axis=0, keepdims=True)

    for n in (4, 3, 2, 1, 0):
        sides(n, backward)
        rs_kv(n)
        if n == 4:
            rs_text(3)
            arrive(AT.at[ox], xs.at[8], xr.at[8])
        if n == 3:
            rs_text(2)
        if n == 2:
            rs_text(1)
        if n == 1:
            rs_text(0)
            push(RT.at[2 * z + ox], FRT, xs.at[9], xr.at[9], partner)
        if n == 0:
            push(R.at[2 * z + ox], FR, xs.at[10], xr.at[10], partner)
            DQ[0] = (FACTOR * DQT[...]).T.astype(BF).reshape(2, TOK, HD)
            push(DQ.at[:, ox], DR, xs.at[11], xr.at[11], partner)
        sides(n, weight_part)
        if n > 0:
            rs_weight(n)

    for side in range(2):
        for unit in range(2):
            arrive(GG.at[side, unit, 0], gs.at[side, unit, 0], gr.at[side, unit, 0])
    stores = []

    def store(src, dst):
        copy = pltpu.make_async_copy(src, dst, st.at[len(stores)])
        copy.start()
        stores.append(copy)

    total = jnp.concatenate(
        [
            GP[z, unit * FEAT : (unit + 1) * FEAT].astype(F32) + GG[0, unit, 0].astype(F32) + GG[1, unit, 0].astype(F32)
            for unit in range(2)
        ],
        axis=0,
    )
    for h in range(2):
        for b in range(2):
            at = (2 * h + b) * HD
            OW[b * HD : (b + 1) * HD, h * HD : (h + 1) * HD] = total[at : at + HD].T
    last = total[4 * HD :].T
    for h in range(2):
        OW[2 * HD : FEAT, h * HD : (h + 1) * HD] = last[h * 64 : (h + 1) * 64]
    store(OW, gw_o)

    arrive(FRT, xs.at[9], xr.at[9])
    arrive(FR, xs.at[10], xr.at[10])
    arrive(DR, xs.at[11], xr.at[11])
    for ref, out, mine, other, at, rows in (
        (OK, gk_o, R, FR, 0, TOK),
        (OV, gv_o, R, FR, TOK, TOK),
        (OTK, gtk_o, RT, FRT, 0, TXT),
        (OTV, gtv_o, RT, FRT, TXT, TXT),
    ):
        ref[:, own_cols] = mine[c, at : at + rows]
        ref[:, other_cols] = other[at : at + rows]
        store(ref, out)
    for n, (ref, out) in enumerate(((OQ, gq_o), (OC, gc_o))):
        ref[:, own_cols] = DQ[n, xh]
        ref[:, other_cols] = DR[n]
        store(ref, out)
    for copy in pending:
        copy.wait_send()

    @pl.when(jnp.logical_not(is_self))
    def _():
        remote(SL, SB.at[xh, j0], s1s.at[0], s1r.at[xlo], s1_same).wait_send()

    for copy in stores:
        copy.wait()


def hand_on(*refs):
    for n in range(7):
        refs[7 + n][...] = refs[n][...]


def local(go, gate, *rest):
    args = (go, gate.T) + rest
    any_spec = pl.BlockSpec(memory_space=pl.ANY)
    smem = pl.BlockSpec(memory_space=pltpu.SMEM)
    in_specs = [any_spec] * 12
    in_specs[2] = in_specs[11] = smem
    outs = [jax.ShapeDtypeStruct((TOK, 2 * HD), BF)] * 4
    outs += [jax.ShapeDtypeStruct((TXT, 2 * HD), BF)] * 2
    outs += [jax.ShapeDtypeStruct((FEAT, 2 * HD), F32)]
    V = pltpu.VMEM
    S = pltpu.SemaphoreType.DMA
    scratch = [
        V((2 * NZ, PAIR, HD), BF),
        V((2 * NZ, 2 * TXT, HD), BF),
        V((2 * TXT, HD), BF),
        V((PAIR, HD), BF),
        V((3, 2, TOK, HD), BF),
        V((3, TOK, HD), BF),
        V((TOK, FEAT), BF),
        V((FEAT, STEPS), F32),
        V((D + FPAD - FEAT, 2 * HD), BF),
        V((PACK, HD), BF),
        V((2, NZ, PACK, HD), BF),
        V((NZ, PAIR, FPAD), BF),
        V((PAIR, HD), BF),
        V((PAIR, HD), BF),
        V((2, HD, PAIR), BF),
        V((2 * NZ, TOK, PAIR), F32),
        V((8, PAIR), F32),
        V((HD, PAIR), F32),
        V((HD, PAIR), F32),
        V((PAIR, HD), F32),
        V((PAIR, 2 * HD), F32),
        V((PAIR, HD), BF),
        V((2 * NZ, PAIR, HD), BF),
        V((2 * NZ, 2 * TXT, HD), BF),
        V((2, 2, 4, PAIR, HD), BF),
        V((2, 2, 4, 2 * TXT, HD), BF),
        V((NZ, 2 * FEAT, HD), BF),
        V((2, 2, 4, FEAT, HD), BF),
        V((PAIR, HD), BF),
        V((2 * TXT, HD), BF),
        V((2, 2, TOK, HD), BF),
        V((2, TOK, HD), BF),
        V((TOK, 2 * HD), BF),
        V((TOK, 2 * HD), BF),
        V((TOK, 2 * HD), BF),
        V((TOK, 2 * HD), BF),
        V((TXT, 2 * HD), BF),
        V((TXT, 2 * HD), BF),
        V((FEAT, 2 * HD), F32),
        S((17,)),
        S((7,)),
        S((12,)),
        S((12,)),
        S((2, 2, 4)),
        S((2, 2, 4)),
        S((2, 2, 4)),
        S((2, 2, 4)),
        S((2,)),
        S((2,)),
        S((2, 2)),
        S((2, 2)),
        S((2,)),
        S((2,)),
        S((4, 2)),
        S((4, 2)),
        S((2, 2, 4)),
        S((2, 2, 4)),
        S((2, 2, 4)),
        S((2, 2, 4)),
        S((2, 2, 4)),
        S((2, 2, 4)),
    ]
    results = pl.pallas_call(
        kernel,
        out_shape=outs,
        in_specs=in_specs,
        out_specs=[any_spec] * 7,
        scratch_shapes=scratch,
        compiler_params=pltpu.CompilerParams(
            collective_id=0, has_side_effects=True, vmem_limit_bytes=56 * 1024 * 1024
        ),
    )(*args)
    return pl.pallas_call(
        hand_on,
        out_shape=outs,
        in_specs=[pl.BlockSpec(memory_space=V)] * 7,
        out_specs=[pl.BlockSpec(memory_space=V)] * 7,
    )(*results)


def solution(mesh):
    return jax.shard_map(
        local,
        mesh=mesh,
        in_specs=(
            P("ctx", "patch"),
            P(None, "patch"),
            P(),
            P(None, "patch"),
            P("ctx", "patch"),
            P("ctx", "patch"),
            P("ctx", "patch"),
            P("ctx", "patch"),
            P("ctx", "patch"),
            P("ctx", "patch"),
            P("ctx", "patch"),
            P(),
        ),
        out_specs=(P("ctx", "patch"),) * 7,
        check_vma=False,
    )
```

```python
import math

import jax
import jax.numpy as jnp
from jax import lax
from jax.experimental import pallas as pl
from jax.experimental.pallas import tpu as pltpu
from jax.sharding import PartitionSpec as P

HD = 128
TOK = 192
PAIR = 2 * TOK
TXT = 32
NZ = 8
FEAT = 320
FPAD = 384
PACK = 2 * TOK + TOK // 2
D = 5120
STEPS = 1000
BF = jnp.bfloat16
F32 = jnp.float32
MESH = pl.DeviceIdType.MESH
FACTOR = 1.0 / math.sqrt(HD)

NN = (((1,), (0,)), ((), ()))
NT = (((1,), (1,)), ((), ()))
TN = (((0,), (0,)), ((), ()))


def mm(a, b, dims):
    return lax.dot_general(a, b, dims, preferred_element_type=F32)


def kernel(
    go_h, gate_h, ts_s, w_h, q_h, k_h, v_h, cq_h, tk_h, tv_h, cg_h, tc_s,
    gq_o, gk_o, gv_o, gc_o, gtk_o, gtv_o, gw_o,
    U, UT, QA, GO, GT, W, SL, SB, SU, GS, GR, AT, ST, STAT, OT, DQT, DO, DW, DOB, R, RT, RR, RRT, GP, GG, FR, FRT, DQ, DR,
    OQ, OK, OV, OC, OTK, OTV, OW,
    ld, st, xs, xr, ags, agr, ats, atr, s1s, s1r, s2s, s2r, s2fs, s2fr, s3s, s3r, ks, kr, ts, tr, gs, gr,
):
    c = lax.axis_index("ctx")
    p = lax.axis_index("patch")
    z, xh = c // 2, lax.rem(c, 2)
    ox = 1 - xh
    y, core, xlo = p // 4, lax.rem(p, 2), lax.rem(p // 2, 2)
    zr = lambda n: lax.rem(z + n + NZ, NZ)
    yr = lambda n: lax.rem(y + n + 4, 4)
    partner = (2 * z + ox, p)
    right = (2 * zr(1) + xh, p)
    left = (2 * zr(-1) + xh, p)
    ydev = [(c, yr(n) * 4 + xlo * 2 + core) for n in (1, -1)]
    sibling = (c, p + 1 - 2 * core)
    s1_same = (2 * z + core, y * 4 + xlo * 2 + xh)
    s1_flip = (2 * z + core, y * 4 + (1 - xlo) * 2 + xh)
    diagonal = (2 * z + ox, sibling[1])
    is_self = core == xh
    own_cols = pl.ds(pl.multiple_of(xh * HD, HD), HD)
    other_cols = pl.ds(pl.multiple_of(ox * HD, HD), HD)

    def remote(src, dst, send, recv, dev):
        return pltpu.make_async_remote_copy(
            src_ref=src, dst_ref=dst, send_sem=send, recv_sem=recv, device_id=dev, device_id_type=MESH
        )

    pending = []

    def push(src, dst, send, recv, dev):
        copy = remote(src, dst, send, recv, dev)
        copy.start()
        pending.append(copy)

    def arrive(dst, send, recv):
        remote(dst, dst, send, recv, partner).wait_recv()

    loads = []

    def load(src, dst):
        copy = pltpu.make_async_copy(src, dst, ld.at[len(loads)])
        copy.start()
        loads.append(copy)

    load(gate_h, GT)
    load(go_h, GO)
    load(tk_h.at[:, own_cols], UT.at[c, pl.ds(0, TXT)])
    load(tv_h.at[:, own_cols], UT.at[c, pl.ds(TXT, TXT)])
    load(k_h.at[:, own_cols], U.at[c, pl.ds(0, TOK)])
    load(v_h.at[:, own_cols], U.at[c, pl.ds(TOK, TOK)])
    for n, src in enumerate((q_h, cq_h, cg_h)):
        load(src.at[:, own_cols], QA.at[n, xh])

    barrier = pltpu.get_barrier_semaphore()
    for dev in [partner, right, left, sibling, s1_flip, diagonal] + ydev:
        pl.semaphore_signal(barrier, inc=1, device_id=dev, device_id_type=MESH)
    W[pl.ds(D, FPAD - FEAT), :] = jnp.zeros((FPAD - FEAT, 2 * HD), BF)
    STAT[...] = jnp.full((8, PAIR), -jnp.inf, F32)
    STAT[1:2, :] = jnp.zeros((1, PAIR), F32)
    OT[...] = jnp.zeros((HD, PAIR), F32)
    DQT[...] = jnp.zeros((HD, PAIR), F32)
    DW[...] = jnp.zeros((PAIR, 2 * HD), F32)
    pl.semaphore_wait(barrier, 8)

    def cross_x(n, src, dst):
        push(src.at[:, other_cols], dst, xs.at[n], xr.at[n], partner)


    def ag_len(stream, side):
        return 4 if stream == side else 3

    def ag_unit(stream, side, n):
        return 2 * (zr(-n) if side == 0 else zr(n)) + (xh if stream == 0 else ox)

    def ag_send(buf, ss, rs, stream, side, n):
        if n < ag_len(stream, side):
            unit = ag_unit(stream, side, n)
            at = (stream, side, n)
            push(buf.at[unit], buf.at[unit], ss.at[at], rs.at[at], right if side == 0 else left)

    def ag_step(buf, ss, rs, stream, n):
        units = []
        for side in range(2):
            if n < ag_len(stream, side):
                unit = ag_unit(stream, side, n + 1)
                arrive(buf.at[unit], ss.at[stream, side, n], rs.at[stream, side, n])
                ag_send(buf, ss, rs, stream, side, n + 1)
                units.append(unit)
        return units

    def text_step(n):
        for stream in range(2):
            ag_step(UT, ats, atr, stream, n)

    block = lambda n, b: SB.at[core, 2 * yr(n) + b]

    def own_block(b):
        for n in range(2):
            push(block(0, b), block(0, b), s2s.at[n, b], s2r.at[n, b], ydev[n])
        push(block(0, b), block(0, b), s3s.at[0, b], s3r.at[0, b], sibling)

    def scaled_own():
        @pl.when(jnp.logical_not(is_self))
        def _():
            arrive(block(0, xlo), s1s.at[0], s1r.at[xlo])

        own_block(xlo)
        arrive(block(0, 1 - xlo), s1s.at[1], s1r.at[1 - xlo])
        own_block(1 - xlo)

    def scaled_near():
        for n in range(2):
            frm = 2 * n - 1
            for b in range(2):
                arrive(block(frm, b), s2s.at[n, b], s2r.at[n, b])
                if b == n:
                    push(block(frm, b), block(frm, b), s2fs.at[n], s2fr.at[n], ydev[n])
                push(block(frm, b), block(frm, b), s3s.at[1 + n, b], s3r.at[1 + n, b], sibling)

    def scaled_far():
        for b in range(2):
            arrive(block(2, b), s2fs.at[b], s2fr.at[b])
            push(block(2, b), block(2, b), s3s.at[3, b], s3r.at[3, b], sibling)

    def stacked(index):
        return QA[index].reshape(PAIR, HD)

    def rows_of(zb, at):
        return jnp.concatenate([U[2 * zb, at : at + TOK], U[2 * zb + 1, at : at + TOK]], axis=0)

    def forward(unit):
        scores = FACTOR * mm(U[unit, 0:TOK], stacked(0), NT)
        ST[unit] = scores
        top = STAT[0:1]
        new_top = jnp.maximum(top, jnp.max(scores, axis=0, keepdims=True))
        decay = jnp.exp(top - new_top)
        probs = jnp.exp(scores - new_top)
        STAT[0:1] = new_top
        STAT[1:2] = STAT[1:2] * decay + jnp.sum(probs, axis=0, keepdims=True)
        OT[...] = OT[...] * decay + mm(U[unit, TOK:PAIR], probs.astype(BF), TN)

    def kv_step(stream, n):
        return ag_step(U, ags, agr, stream, n)

    def forward_all(units):
        for unit in units:
            forward(unit)

    def rs_len(side, unit):
        return 4 if side == unit else 3

    def rs_step(n, cur, slots, ss, rs, units=(0, 1)):
        for side in range(2):
            dest = zr(n) if side == 0 else zr(-n)
            dev = right if side == 0 else left
            for unit in units:
                length = rs_len(side, unit)
                ref = cur(dest, unit)
                if n < length:
                    slot = slots.at[side, unit, n]
                    arrive(slot, ss.at[side, unit, n], rs.at[side, unit, n])
                    ref[...] = (ref[...].astype(F32) + slot[...].astype(F32)).astype(BF)
                if 0 < n <= length:
                    push(ref, slots.at[side, unit, n - 1], ss.at[side, unit, n - 1], rs.at[side, unit, n - 1], dev)

    def rs_text(n):
        rs_step(n, lambda dest, unit: RT.at[2 * dest + unit], RRT, ts, tr)

    def rs_kv(n):
        rs_step(n, lambda dest, unit: R.at[2 * dest + unit], RR, ks, kr)

    def rs_weight(stream, n):
        sides(n, weight_part(stream))
        rs_step(n, lambda dest, unit: GP.at[dest, xh if unit == 0 else ox], GG, gs, gr, (stream,))

    def weight_end(stream):
        sides(0, weight_part(stream))
        head, cols = (xh, own_cols) if stream == 0 else (ox, other_cols)
        total = GP[z, head].astype(F32)
        for side in range(2):
            arrive(GG.at[side, stream, 0], gs.at[side, stream, 0], gr.at[side, stream, 0])
            total = total + GG[side, stream, 0].astype(F32)
        OW[0:HD, cols] = total[0:HD].T
        OW[HD : 2 * HD, cols] = total[HD : 2 * HD].T
        rest = total[2 * HD :]
        OW[2 * HD :, cols] = jnp.concatenate([rest[:, : HD // 2], rest[:, HD // 2 :]], axis=0).T

    def text():
        tkeys = UT[:, 0:TXT, :].reshape(2 * NZ * TXT, HD)
        tvalues = UT[:, TXT:, :].reshape(2 * NZ * TXT, HD)
        cgrad, cquery = stacked(2), stacked(1)
        tscores = FACTOR * mm(tkeys, cquery, NT)
        live = lax.broadcasted_iota(jnp.int32, (2 * NZ * TXT, 1), 0) < tc_s[0]
        tscores = jnp.where(live, tscores, -jnp.inf)
        ttop = jnp.max(tscores, axis=0, keepdims=True)
        tmass = ttop + jnp.log(jnp.sum(jnp.exp(tscores - ttop), axis=0, keepdims=True))
        tprobs = jnp.exp(tscores - tmass).astype(BF)
        tgrad_probs = mm(tvalues, cgrad, NT)
        tdelta = jnp.sum(cgrad.astype(F32).T * mm(tvalues, tprobs, TN), axis=0, keepdims=True)
        tgrad_scores = (tprobs.astype(F32) * (tgrad_probs - tdelta)).astype(BF)
        RT[:, 0:TXT, :] = (FACTOR * mm(tgrad_scores, cquery, NN)).astype(BF).reshape(2 * NZ, TXT, HD)
        RT[:, TXT:, :] = mm(tprobs, cgrad, NN).astype(BF).reshape(2 * NZ, TXT, HD)
        dcross = FACTOR * mm(tkeys, tgrad_scores, TN)
        DQ[1] = dcross.T.astype(BF).reshape(2, TOK, HD)
        push(DQ.at[1, ox], DR.at[1], xs.at[11], xr.at[11], partner)

    def project_part(frm, n):
        for b in range(2):
            arrive(SB.at[1 - core, 2 * yr(frm) + b], s3s.at[n, b], s3r.at[n, b])

        def part(b, carry):
            j = 2 * yr(frm) + b
            rows = []
            for s in range(2):
                rest = SB[s, j, PAIR:PACK]
                rest = jnp.concatenate([rest[:, : HD // 2], rest[:, HD // 2 :]], axis=0)
                rows.append(
                    jnp.concatenate([SB[s, j, 0:TOK], SB[s, j, TOK:PAIR], rest, jnp.zeros((TOK, HD // 2), BF)], axis=1)
                )
            rows = jnp.concatenate(rows, axis=0)
            SU[j] = rows
            weight = W[pl.ds(pl.multiple_of(FEAT * (2 * j + xh), 64), FPAD), :]
            DW[...] = DW[...] + mm(rows, weight, NN)
            return carry

        lax.fori_loop(0, 2, part, 0)

    def project_end():
        low, high = DW[:, :HD], DW[:, HD:]
        mine = xh == 0
        GS[...] = jnp.where(mine, high, low).astype(BF)
        push(GS, GR, xs.at[7], xr.at[7], partner)
        DO[...] = jnp.where(mine, low, high)

    def backward(zb):
        keys, vals = rows_of(zb, 0), rows_of(zb, TOK)
        out_grad = DOB[...]
        scores = ST[pl.ds(2 * zb, 2)].reshape(PAIR, PAIR)
        probs = jnp.exp(scores - STAT[2:3]).astype(BF)
        grad_scores = (probs.astype(F32) * (mm(vals, out_grad, NT) - STAT[3:4])).astype(BF)
        dvals = mm(probs, out_grad, NN).astype(BF)
        dkeys = (FACTOR * mm(grad_scores, stacked(0), NN)).astype(BF)
        DQT[...] = DQT[...] + mm(keys, grad_scores, TN)
        for s in range(2):
            R[2 * zb + s, 0:TOK] = dkeys[s * TOK : (s + 1) * TOK]
            R[2 * zb + s, TOK:PAIR] = dvals[s * TOK : (s + 1) * TOK]

    def weight_part(stream):
        head = xh if stream == 0 else ox

        def one(j):
            part = mm(AT[head], SU[j], NN).astype(BF)
            GP[j, head, 0:HD] = part[:, 0:HD]
            GP[j, head, HD : 2 * HD] = part[:, HD : 2 * HD]
            GP[j, head, 2 * HD :] = jnp.concatenate([part[: HD // 2, 2 * HD : FEAT], part[HD // 2 :, 2 * HD : FEAT]], axis=1)

        return one

    def sides(n, step):
        if n in (0, 4):
            step(zr(n))
        else:

            def one(side, carry):
                step(zr((1 - 2 * side) * n))
                return carry

            lax.fori_loop(0, 2, one, 0)

    cross_x(0, tk_h, UT.at[c, pl.ds(0, TXT)])
    cross_x(1, tv_h, UT.at[c, pl.ds(TXT, TXT)])
    cross_x(2, k_h, U.at[c, pl.ds(0, TOK)])
    cross_x(3, v_h, U.at[c, pl.ds(TOK, TOK)])
    cross_x(4, q_h, QA.at[0, xh])
    loads[2].wait()
    loads[3].wait()
    for side in range(2):
        ag_send(UT, ats, atr, 0, side, 0)
    loads[4].wait()
    loads[5].wait()
    for side in range(2):
        ag_send(U, ags, agr, 0, side, 0)

    loads[0].wait()
    loads[1].wait()
    chosen = lax.broadcasted_iota(jnp.int32, (1, STEPS), 1) == ts_s[0]
    gate_col = jnp.sum(jnp.where(chosen, GT[...], 0.0), axis=1, keepdims=True)
    gate_row = jnp.broadcast_to(gate_col, (FEAT, HD)).T[0:1]
    scaled = (gate_row * GO[...].astype(F32)).astype(BF)
    SL[0:TOK] = scaled[:, :HD]
    SL[TOK:PAIR] = scaled[:, HD : 2 * HD]
    SL[PAIR:PACK] = jnp.concatenate([scaled[: TOK // 2, 2 * HD :], scaled[TOK // 2 :, 2 * HD :]], axis=1)
    j0 = 2 * y + xlo
    push(SL, SB.at[xh, j0], s1s.at[1], s1r.at[xlo], s1_flip)

    @pl.when(is_self)
    def _():
        SB[xh, j0] = SL[...]

    @pl.when(jnp.logical_not(is_self))
    def _():
        remote(SL, SB.at[xh, j0], s1s.at[0], s1r.at[xlo], s1_same).start()

    load(w_h, W.at[pl.ds(0, D)])

    arrive(UT.at[2 * z + ox, pl.ds(0, TXT)], xs.at[0], xr.at[0])
    arrive(UT.at[2 * z + ox, pl.ds(TXT, TXT)], xs.at[1], xr.at[1])
    for side in range(2):
        ag_send(UT, ats, atr, 1, side, 0)
    for n in range(2):
        arrive(U.at[2 * z + ox, pl.ds(n * TOK, TOK)], xs.at[2 + n], xr.at[2 + n])
    for side in range(2):
        ag_send(U, ags, agr, 1, side, 0)

    a0 = kv_step(0, 0)
    scaled_own()
    cross_x(5, cq_h, QA.at[1, xh])
    cross_x(6, cg_h, QA.at[2, xh])
    b0 = kv_step(1, 0)
    loads[6].wait()
    arrive(QA.at[0, ox], xs.at[4], xr.at[4])
    forward_all([c, 2 * z + ox] + a0 + b0)
    a1 = kv_step(0, 1)
    text_step(0)
    forward_all(a1)
    b1 = kv_step(1, 1)
    forward_all(b1)
    scaled_near()
    a2 = kv_step(0, 2)
    text_step(1)
    forward_all(a2)
    scaled_far()
    b2 = kv_step(1, 2)
    text_step(2)
    loads[9].wait()
    project_part(0, 0)
    project_part(-1, 1)
    project_part(1, 2)
    project_part(2, 3)
    project_end()
    forward_all(b2)
    a3 = kv_step(0, 3)
    text_step(3)
    forward_all(a3)
    b3 = kv_step(1, 3)
    forward_all(b3)
    mass = STAT[1:2]
    OT[...] = OT[...] / mass
    AT[xh] = OT[...].astype(BF)
    push(AT.at[xh], AT.at[xh], xs.at[8], xr.at[8], partner)
    STAT[2:3] = STAT[0:1] + jnp.log(mass)
    arrive(GR, xs.at[7], xr.at[7])
    DO[...] = DO[...] + GR[...].astype(F32)
    DOB[...] = DO[...].astype(BF)
    STAT[3:4] = jnp.sum(DOB[...].astype(F32).T * OT[...], axis=0, keepdims=True)
    backward(zr(4))
    rs_kv(4)
    rs_weight(0, 4)
    loads[7].wait()
    loads[8].wait()
    arrive(QA.at[1, ox], xs.at[5], xr.at[5])
    arrive(QA.at[2, ox], xs.at[6], xr.at[6])
    text()
    rs_text(4)
    arrive(AT.at[ox], xs.at[8], xr.at[8])
    rs_weight(1, 4)
    sides(3, backward)
    rs_kv(3)
    rs_weight(0, 3)
    rs_weight(1, 3)
    rs_text(3)
    sides(2, backward)
    backward(z)
    rs_kv(2)
    rs_weight(0, 2)
    rs_weight(1, 2)
    rs_text(2)
    sides(1, backward)
    DQ[0] = (FACTOR * DQT[...]).T.astype(BF).reshape(2, TOK, HD)
    push(DQ.at[0, ox], DR.at[0], xs.at[12], xr.at[12], partner)
    rs_kv(1)
    rs_text(1)
    rs_weight(0, 1)
    rs_weight(1, 1)
    rs_kv(0)
    push(R.at[2 * z + ox], FR, xs.at[10], xr.at[10], partner)
    rs_text(0)
    push(RT.at[2 * z + ox], FRT, xs.at[9], xr.at[9], partner)
    weight_end(0)
    weight_end(1)

    stores = []

    def store(src, dst):
        copy = pltpu.make_async_copy(src, dst, st.at[len(stores)])
        copy.start()
        stores.append(copy)

    store(OW, gw_o)

    arrive(FRT, xs.at[9], xr.at[9])
    arrive(FR, xs.at[10], xr.at[10])
    arrive(DR.at[1], xs.at[11], xr.at[11])
    arrive(DR.at[0], xs.at[12], xr.at[12])
    for ref, out, mine, other, at, rows in (
        (OK, gk_o, R, FR, 0, TOK),
        (OV, gv_o, R, FR, TOK, TOK),
        (OTK, gtk_o, RT, FRT, 0, TXT),
        (OTV, gtv_o, RT, FRT, TXT, TXT),
    ):
        ref[:, own_cols] = mine[c, at : at + rows]
        ref[:, other_cols] = other[at : at + rows]
        store(ref, out)
    for n, (ref, out) in enumerate(((OQ, gq_o), (OC, gc_o))):
        ref[:, own_cols] = DQ[n, xh]
        ref[:, other_cols] = DR[n]
        store(ref, out)
    for copy in pending:
        copy.wait_send()

    @pl.when(jnp.logical_not(is_self))
    def _():
        remote(SL, SB.at[xh, j0], s1s.at[0], s1r.at[xlo], s1_same).wait_send()

    for copy in stores:
        copy.wait()


def hand_on(*refs):
    for n in range(7):
        refs[7 + n][...] = refs[n][...]


def local(go, gate, *rest):
    args = (go, gate.T) + rest
    any_spec = pl.BlockSpec(memory_space=pl.ANY)
    smem = pl.BlockSpec(memory_space=pltpu.SMEM)
    in_specs = [any_spec] * 12
    in_specs[2] = in_specs[11] = smem
    outs = [jax.ShapeDtypeStruct((TOK, 2 * HD), BF)] * 4
    outs += [jax.ShapeDtypeStruct((TXT, 2 * HD), BF)] * 2
    outs += [jax.ShapeDtypeStruct((FEAT, 2 * HD), F32)]
    V = pltpu.VMEM
    S = pltpu.SemaphoreType.DMA
    scratch = [
        V((2 * NZ, PAIR, HD), BF),
        V((2 * NZ, 2 * TXT, HD), BF),
        V((3, 2, TOK, HD), BF),
        V((TOK, FEAT), BF),
        V((FEAT, STEPS), F32),
        V((D + FPAD - FEAT, 2 * HD), BF),
        V((PACK, HD), BF),
        V((2, NZ, PACK, HD), BF),
        V((NZ, PAIR, FPAD), BF),
        V((PAIR, HD), BF),
        V((PAIR, HD), BF),
        V((2, HD, PAIR), BF),
        V((2 * NZ, TOK, PAIR), F32),
        V((8, PAIR), F32),
        V((HD, PAIR), F32),
        V((HD, PAIR), F32),
        V((PAIR, HD), F32),
        V((PAIR, 2 * HD), F32),
        V((PAIR, HD), BF),
        V((2 * NZ, PAIR, HD), BF),
        V((2 * NZ, 2 * TXT, HD), BF),
        V((2, 2, 4, PAIR, HD), BF),
        V((2, 2, 4, 2 * TXT, HD), BF),
        V((NZ, 2, FEAT, HD), BF),
        V((2, 2, 4, FEAT, HD), BF),
        V((PAIR, HD), BF),
        V((2 * TXT, HD), BF),
        V((2, 2, TOK, HD), BF),
        V((2, TOK, HD), BF),
        V((TOK, 2 * HD), BF),
        V((TOK, 2 * HD), BF),
        V((TOK, 2 * HD), BF),
        V((TOK, 2 * HD), BF),
        V((TXT, 2 * HD), BF),
        V((TXT, 2 * HD), BF),
        V((FEAT, 2 * HD), F32),
        S((10,)),
        S((7,)),
        S((13,)),
        S((13,)),
        S((2, 2, 4)),
        S((2, 2, 4)),
        S((2, 2, 4)),
        S((2, 2, 4)),
        S((2,)),
        S((2,)),
        S((2, 2)),
        S((2, 2)),
        S((2,)),
        S((2,)),
        S((4, 2)),
        S((4, 2)),
        S((2, 2, 4)),
        S((2, 2, 4)),
        S((2, 2, 4)),
        S((2, 2, 4)),
        S((2, 2, 4)),
        S((2, 2, 4)),
    ]
    results = pl.pallas_call(
        kernel,
        out_shape=outs,
        in_specs=in_specs,
        out_specs=[any_spec] * 7,
        scratch_shapes=scratch,
        compiler_params=pltpu.CompilerParams(
            collective_id=0, has_side_effects=True, vmem_limit_bytes=56 * 1024 * 1024
        ),
    )(*args)
    return pl.pallas_call(
        hand_on,
        out_shape=outs,
        in_specs=[pl.BlockSpec(memory_space=V)] * 7,
        out_specs=[pl.BlockSpec(memory_space=V)] * 7,
    )(*results)


def solution(mesh):
    return jax.shard_map(
        local,
        mesh=mesh,
        in_specs=(
            P("ctx", "patch"),
            P(None, "patch"),
            P(),
            P(None, "patch"),
            P("ctx", "patch"),
            P("ctx", "patch"),
            P("ctx", "patch"),
            P("ctx", "patch"),
            P("ctx", "patch"),
            P("ctx", "patch"),
            P("ctx", "patch"),
            P(),
        ),
        out_specs=(P("ctx", "patch"),) * 7,
        check_vma=False,
    )
```

```python
import math

import jax
import jax.numpy as jnp
from jax import lax
from jax.experimental import pallas as pl
from jax.experimental.pallas import tpu as pltpu
from jax.sharding import PartitionSpec as P

HD = 128
TOK = 192
PAIR = 2 * TOK
TXT = 32
NZ = 8
FEAT = 320
FPAD = 384
PACK = 2 * TOK + TOK // 2
D = 5120
STEPS = 1000
BF = jnp.bfloat16
F32 = jnp.float32
MESH = pl.DeviceIdType.MESH
FACTOR = 1.0 / math.sqrt(HD)

NN = (((1,), (0,)), ((), ()))
NT = (((1,), (1,)), ((), ()))
TN = (((0,), (0,)), ((), ()))


def mm(a, b, dims):
    return lax.dot_general(a, b, dims, preferred_element_type=F32)


def kernel(
    go_h, gate_h, ts_s, w_h, q_h, k_h, v_h, cq_h, tk_h, tv_h, cg_h, tc_s,
    OQ, OK, OV, OC, OTK, OTV, OW,
    U, UT, QA, GO, GT, W, SL, SB, SU, GS, GR, AT, ST, STAT, OT, DQT, DO, DW, DOB, R, RT, RR, RRT, GP, GG, FR, FRT, DQ, DR,
    ld, xs, xr, ags, agr, ats, atr, s1s, s1r, s2s, s2r, s2fs, s2fr, s3s, s3r, ks, kr, ts, tr, gs, gr,
):
    c = lax.axis_index("ctx")
    p = lax.axis_index("patch")
    z, xh = c // 2, lax.rem(c, 2)
    ox = 1 - xh
    y, core, xlo = p // 4, lax.rem(p, 2), lax.rem(p // 2, 2)
    zr = lambda n: lax.rem(z + n + NZ, NZ)
    yr = lambda n: lax.rem(y + n + 4, 4)
    partner = (2 * z + ox, p)
    right = (2 * zr(1) + xh, p)
    left = (2 * zr(-1) + xh, p)
    ydev = [(c, yr(n) * 4 + xlo * 2 + core) for n in (1, -1)]
    sibling = (c, p + 1 - 2 * core)
    s1_same = (2 * z + core, y * 4 + xlo * 2 + xh)
    s1_flip = (2 * z + core, y * 4 + (1 - xlo) * 2 + xh)
    diagonal = (2 * z + ox, sibling[1])
    is_self = core == xh
    own_cols = pl.ds(pl.multiple_of(xh * HD, HD), HD)
    other_cols = pl.ds(pl.multiple_of(ox * HD, HD), HD)

    def remote(src, dst, send, recv, dev):
        return pltpu.make_async_remote_copy(
            src_ref=src, dst_ref=dst, send_sem=send, recv_sem=recv, device_id=dev, device_id_type=MESH
        )

    pending = []

    def push(src, dst, send, recv, dev):
        copy = remote(src, dst, send, recv, dev)
        copy.start()
        pending.append(copy)

    def arrive(dst, send, recv):
        remote(dst, dst, send, recv, partner).wait_recv()

    loads = []

    def load(src, dst):
        copy = pltpu.make_async_copy(src, dst, ld.at[len(loads)])
        copy.start()
        loads.append(copy)

    load(tk_h.at[:, own_cols], UT.at[c, pl.ds(0, TXT)])
    load(tv_h.at[:, own_cols], UT.at[c, pl.ds(TXT, TXT)])
    load(k_h.at[:, own_cols], U.at[c, pl.ds(0, TOK)])
    load(v_h.at[:, own_cols], U.at[c, pl.ds(TOK, TOK)])
    load(gate_h, GT)
    load(go_h, GO)
    for n, src in enumerate((q_h, cq_h, cg_h)):
        load(src.at[:, own_cols], QA.at[n, xh])

    barrier = pltpu.get_barrier_semaphore()
    for dev in [partner, right, left, sibling, s1_flip, diagonal] + ydev:
        pl.semaphore_signal(barrier, inc=1, device_id=dev, device_id_type=MESH)
    W[pl.ds(D, FPAD - FEAT), :] = jnp.zeros((FPAD - FEAT, 2 * HD), BF)
    STAT[...] = jnp.full((8, PAIR), -jnp.inf, F32)
    STAT[1:2, :] = jnp.zeros((1, PAIR), F32)
    OT[...] = jnp.zeros((HD, PAIR), F32)
    DQT[...] = jnp.zeros((HD, PAIR), F32)
    DW[...] = jnp.zeros((PAIR, 2 * HD), F32)
    pl.semaphore_wait(barrier, 8)

    def cross_x(n, src, dst):
        push(src.at[:, other_cols], dst, xs.at[n], xr.at[n], partner)


    def ag_len(stream, side):
        return 4 if stream == side else 3

    def ag_unit(stream, side, n):
        return 2 * (zr(-n) if side == 0 else zr(n)) + (xh if stream == 0 else ox)

    def ag_send(buf, ss, rs, stream, side, n):
        if n < ag_len(stream, side):
            unit = ag_unit(stream, side, n)
            at = (stream, side, n)
            push(buf.at[unit], buf.at[unit], ss.at[at], rs.at[at], right if side == 0 else left)

    def ag_step(buf, ss, rs, stream, n):
        units = []
        for side in range(2):
            if n < ag_len(stream, side):
                unit = ag_unit(stream, side, n + 1)
                arrive(buf.at[unit], ss.at[stream, side, n], rs.at[stream, side, n])
                ag_send(buf, ss, rs, stream, side, n + 1)
                units.append(unit)
        return units

    def text_step(n):
        for stream in range(2):
            ag_step(UT, ats, atr, stream, n)

    block = lambda n, b: SB.at[core, 2 * yr(n) + b]

    def own_block(b):
        for n in range(2):
            push(block(0, b), block(0, b), s2s.at[n, b], s2r.at[n, b], ydev[n])
        push(block(0, b), block(0, b), s3s.at[0, b], s3r.at[0, b], sibling)

    def scaled_own():
        @pl.when(jnp.logical_not(is_self))
        def _():
            arrive(block(0, xlo), s1s.at[0], s1r.at[xlo])

        own_block(xlo)
        arrive(block(0, 1 - xlo), s1s.at[1], s1r.at[1 - xlo])
        own_block(1 - xlo)

    def scaled_near():
        for n in range(2):
            frm = 2 * n - 1
            for b in range(2):
                arrive(block(frm, b), s2s.at[n, b], s2r.at[n, b])
                if b == n:
                    push(block(frm, b), block(frm, b), s2fs.at[n], s2fr.at[n], ydev[n])
                push(block(frm, b), block(frm, b), s3s.at[1 + n, b], s3r.at[1 + n, b], sibling)

    def scaled_far():
        for b in range(2):
            arrive(block(2, b), s2fs.at[b], s2fr.at[b])
            push(block(2, b), block(2, b), s3s.at[3, b], s3r.at[3, b], sibling)

    def stacked(index):
        return QA[index].reshape(PAIR, HD)

    def rows_of(zb, at):
        return jnp.concatenate([U[2 * zb, at : at + TOK], U[2 * zb + 1, at : at + TOK]], axis=0)

    def forward(unit):
        scores = FACTOR * mm(U[unit, 0:TOK], stacked(0), NT)
        ST[unit] = scores
        top = STAT[0:1]
        new_top = jnp.maximum(top, jnp.max(scores, axis=0, keepdims=True))
        decay = jnp.exp(top - new_top)
        probs = jnp.exp(scores - new_top)
        STAT[0:1] = new_top
        STAT[1:2] = STAT[1:2] * decay + jnp.sum(probs, axis=0, keepdims=True)
        OT[...] = OT[...] * decay + mm(U[unit, TOK:PAIR], probs.astype(BF), TN)

    def kv_step(stream, n):
        return ag_step(U, ags, agr, stream, n)

    def forward_all(units):
        for unit in units:
            forward(unit)

    def rs_len(side, unit):
        return 4 if side == unit else 3

    def rs_step(n, cur, slots, ss, rs, units=(0, 1)):
        for side in range(2):
            dest = zr(n) if side == 0 else zr(-n)
            dev = right if side == 0 else left
            for unit in units:
                length = rs_len(side, unit)
                ref = cur(dest, unit)
                if n < length:
                    slot = slots.at[side, unit, n]
                    arrive(slot, ss.at[side, unit, n], rs.at[side, unit, n])
                    ref[...] = (ref[...].astype(F32) + slot[...].astype(F32)).astype(BF)
                if 0 < n <= length:
                    push(ref, slots.at[side, unit, n - 1], ss.at[side, unit, n - 1], rs.at[side, unit, n - 1], dev)

    def rs_text(n):
        rs_step(n, lambda dest, unit: RT.at[2 * dest + unit], RRT, ts, tr)

    def rs_kv(n):
        rs_step(n, lambda dest, unit: R.at[2 * dest + unit], RR, ks, kr)

    def rs_weight(stream, n):
        sides(n, weight_part(stream))
        rs_step(n, lambda dest, unit: GP.at[dest, xh if unit == 0 else ox], GG, gs, gr, (stream,))

    def weight_end(stream):
        sides(0, weight_part(stream))
        head, cols = (xh, own_cols) if stream == 0 else (ox, other_cols)
        total = GP[z, head].astype(F32)
        for side in range(2):
            arrive(GG.at[side, stream, 0], gs.at[side, stream, 0], gr.at[side, stream, 0])
            total = total + GG[side, stream, 0].astype(F32)
        OW[0:HD, cols] = total[0:HD].T
        OW[HD : 2 * HD, cols] = total[HD : 2 * HD].T
        rest = total[2 * HD :]
        OW[2 * HD :, cols] = jnp.concatenate([rest[:, : HD // 2], rest[:, HD // 2 :]], axis=0).T

    def text():
        tkeys = UT[:, 0:TXT, :].reshape(2 * NZ * TXT, HD)
        tvalues = UT[:, TXT:, :].reshape(2 * NZ * TXT, HD)
        cgrad, cquery = stacked(2), stacked(1)
        tscores = FACTOR * mm(tkeys, cquery, NT)
        live = lax.broadcasted_iota(jnp.int32, (2 * NZ * TXT, 1), 0) < tc_s[0]
        tscores = jnp.where(live, tscores, -jnp.inf)
        ttop = jnp.max(tscores, axis=0, keepdims=True)
        tmass = ttop + jnp.log(jnp.sum(jnp.exp(tscores - ttop), axis=0, keepdims=True))
        tprobs = jnp.exp(tscores - tmass).astype(BF)
        tgrad_probs = mm(tvalues, cgrad, NT)
        tdelta = jnp.sum(cgrad.astype(F32).T * mm(tvalues, tprobs, TN), axis=0, keepdims=True)
        tgrad_scores = (tprobs.astype(F32) * (tgrad_probs - tdelta)).astype(BF)
        RT[:, 0:TXT, :] = (FACTOR * mm(tgrad_scores, cquery, NN)).astype(BF).reshape(2 * NZ, TXT, HD)
        RT[:, TXT:, :] = mm(tprobs, cgrad, NN).astype(BF).reshape(2 * NZ, TXT, HD)
        dcross = FACTOR * mm(tkeys, tgrad_scores, TN)
        DQ[1] = dcross.T.astype(BF).reshape(2, TOK, HD)
        push(DQ.at[1, ox], DR.at[1], xs.at[11], xr.at[11], partner)

    def project_part(frm, n):
        for b in range(2):
            arrive(SB.at[1 - core, 2 * yr(frm) + b], s3s.at[n, b], s3r.at[n, b])

        def part(b, carry):
            j = 2 * yr(frm) + b
            rows = []
            for s in range(2):
                rest = SB[s, j, PAIR:PACK]
                rest = jnp.concatenate([rest[:, : HD // 2], rest[:, HD // 2 :]], axis=0)
                rows.append(
                    jnp.concatenate([SB[s, j, 0:TOK], SB[s, j, TOK:PAIR], rest, jnp.zeros((TOK, HD // 2), BF)], axis=1)
                )
            rows = jnp.concatenate(rows, axis=0)
            SU[j] = rows
            weight = W[pl.ds(pl.multiple_of(FEAT * (2 * j + xh), 64), FPAD), :]
            DW[...] = DW[...] + mm(rows, weight, NN)
            return carry

        lax.fori_loop(0, 2, part, 0)

    def project_end():
        low, high = DW[:, :HD], DW[:, HD:]
        mine = xh == 0
        GS[...] = jnp.where(mine, high, low).astype(BF)
        push(GS, GR, xs.at[7], xr.at[7], partner)
        DO[...] = jnp.where(mine, low, high)

    def backward(zb):
        keys, vals = rows_of(zb, 0), rows_of(zb, TOK)
        out_grad = DOB[...]
        scores = ST[pl.ds(2 * zb, 2)].reshape(PAIR, PAIR)
        probs = jnp.exp(scores - STAT[2:3]).astype(BF)
        grad_scores = (probs.astype(F32) * (mm(vals, out_grad, NT) - STAT[3:4])).astype(BF)
        dvals = mm(probs, out_grad, NN).astype(BF)
        dkeys = (FACTOR * mm(grad_scores, stacked(0), NN)).astype(BF)
        DQT[...] = DQT[...] + mm(keys, grad_scores, TN)
        for s in range(2):
            R[2 * zb + s, 0:TOK] = dkeys[s * TOK : (s + 1) * TOK]
            R[2 * zb + s, TOK:PAIR] = dvals[s * TOK : (s + 1) * TOK]

    def weight_part(stream):
        head = xh if stream == 0 else ox

        def one(j):
            part = mm(AT[head], SU[j], NN).astype(BF)
            GP[j, head, 0:HD] = part[:, 0:HD]
            GP[j, head, HD : 2 * HD] = part[:, HD : 2 * HD]
            GP[j, head, 2 * HD :] = jnp.concatenate([part[: HD // 2, 2 * HD : FEAT], part[HD // 2 :, 2 * HD : FEAT]], axis=1)

        return one

    def sides(n, step):
        if n in (0, 4):
            step(zr(n))
        else:

            def one(side, carry):
                step(zr((1 - 2 * side) * n))
                return carry

            lax.fori_loop(0, 2, one, 0)

    cross_x(0, tk_h, UT.at[c, pl.ds(0, TXT)])
    cross_x(1, tv_h, UT.at[c, pl.ds(TXT, TXT)])
    cross_x(2, k_h, U.at[c, pl.ds(0, TOK)])
    cross_x(3, v_h, U.at[c, pl.ds(TOK, TOK)])
    cross_x(4, q_h, QA.at[0, xh])
    loads[0].wait()
    loads[1].wait()
    for side in range(2):
        ag_send(UT, ats, atr, 0, side, 0)
    loads[2].wait()
    loads[3].wait()
    for side in range(2):
        ag_send(U, ags, agr, 0, side, 0)

    loads[4].wait()
    loads[5].wait()
    chosen = lax.broadcasted_iota(jnp.int32, (1, STEPS), 1) == ts_s[0]
    gate_col = jnp.sum(jnp.where(chosen, GT[...], 0.0), axis=1, keepdims=True)
    gate_row = jnp.broadcast_to(gate_col, (FEAT, HD)).T[0:1]
    scaled = (gate_row * GO[...].astype(F32)).astype(BF)
    SL[0:TOK] = scaled[:, :HD]
    SL[TOK:PAIR] = scaled[:, HD : 2 * HD]
    SL[PAIR:PACK] = jnp.concatenate([scaled[: TOK // 2, 2 * HD :], scaled[TOK // 2 :, 2 * HD :]], axis=1)
    j0 = 2 * y + xlo
    push(SL, SB.at[xh, j0], s1s.at[1], s1r.at[xlo], s1_flip)

    @pl.when(is_self)
    def _():
        SB[xh, j0] = SL[...]

    @pl.when(jnp.logical_not(is_self))
    def _():
        remote(SL, SB.at[xh, j0], s1s.at[0], s1r.at[xlo], s1_same).start()

    load(w_h, W.at[pl.ds(0, D)])

    arrive(UT.at[2 * z + ox, pl.ds(0, TXT)], xs.at[0], xr.at[0])
    arrive(UT.at[2 * z + ox, pl.ds(TXT, TXT)], xs.at[1], xr.at[1])
    for side in range(2):
        ag_send(UT, ats, atr, 1, side, 0)
    for n in range(2):
        arrive(U.at[2 * z + ox, pl.ds(n * TOK, TOK)], xs.at[2 + n], xr.at[2 + n])
    for side in range(2):
        ag_send(U, ags, agr, 1, side, 0)

    a0 = kv_step(0, 0)
    scaled_own()
    cross_x(5, cq_h, QA.at[1, xh])
    cross_x(6, cg_h, QA.at[2, xh])
    b0 = kv_step(1, 0)
    loads[6].wait()
    arrive(QA.at[0, ox], xs.at[4], xr.at[4])
    forward_all([c, 2 * z + ox] + a0 + b0)
    a1 = kv_step(0, 1)
    text_step(0)
    forward_all(a1)
    b1 = kv_step(1, 1)
    forward_all(b1)
    scaled_near()
    a2 = kv_step(0, 2)
    text_step(1)
    forward_all(a2)
    scaled_far()
    b2 = kv_step(1, 2)
    text_step(2)
    loads[9].wait()
    project_part(0, 0)
    project_part(-1, 1)
    project_part(1, 2)
    project_part(2, 3)
    project_end()
    forward_all(b2)
    a3 = kv_step(0, 3)
    text_step(3)
    forward_all(a3)
    b3 = kv_step(1, 3)
    forward_all(b3)
    mass = STAT[1:2]
    OT[...] = OT[...] / mass
    AT[xh] = OT[...].astype(BF)
    push(AT.at[xh], AT.at[xh], xs.at[8], xr.at[8], partner)
    STAT[2:3] = STAT[0:1] + jnp.log(mass)
    arrive(GR, xs.at[7], xr.at[7])
    DO[...] = DO[...] + GR[...].astype(F32)
    DOB[...] = DO[...].astype(BF)
    STAT[3:4] = jnp.sum(DOB[...].astype(F32).T * OT[...], axis=0, keepdims=True)
    backward(zr(4))
    rs_kv(4)
    rs_weight(0, 4)
    loads[7].wait()
    loads[8].wait()
    arrive(QA.at[1, ox], xs.at[5], xr.at[5])
    arrive(QA.at[2, ox], xs.at[6], xr.at[6])
    text()
    rs_text(4)
    arrive(AT.at[ox], xs.at[8], xr.at[8])
    rs_weight(1, 4)
    sides(3, backward)
    rs_kv(3)
    rs_weight(0, 3)
    rs_weight(1, 3)
    rs_text(3)
    sides(2, backward)
    backward(z)
    rs_kv(2)
    rs_weight(0, 2)
    rs_weight(1, 2)
    rs_text(2)
    sides(1, backward)
    DQ[0] = (FACTOR * DQT[...]).T.astype(BF).reshape(2, TOK, HD)
    push(DQ.at[0, ox], DR.at[0], xs.at[12], xr.at[12], partner)
    rs_kv(1)
    rs_text(1)
    rs_weight(0, 1)
    rs_weight(1, 1)
    rs_kv(0)
    push(R.at[2 * z + ox], FR, xs.at[10], xr.at[10], partner)
    rs_text(0)
    push(RT.at[2 * z + ox], FRT, xs.at[9], xr.at[9], partner)
    weight_end(0)
    weight_end(1)

    arrive(FRT, xs.at[9], xr.at[9])
    arrive(FR, xs.at[10], xr.at[10])
    arrive(DR.at[1], xs.at[11], xr.at[11])
    arrive(DR.at[0], xs.at[12], xr.at[12])
    for ref, mine, other, at, rows in (
        (OK, R, FR, 0, TOK),
        (OV, R, FR, TOK, TOK),
        (OTK, RT, FRT, 0, TXT),
        (OTV, RT, FRT, TXT, TXT),
    ):
        ref[:, own_cols] = mine[c, at : at + rows]
        ref[:, other_cols] = other[at : at + rows]
    for n, ref in enumerate((OQ, OC)):
        ref[:, own_cols] = DQ[n, xh]
        ref[:, other_cols] = DR[n]
    for copy in pending:
        copy.wait_send()

    @pl.when(jnp.logical_not(is_self))
    def _():
        remote(SL, SB.at[xh, j0], s1s.at[0], s1r.at[xlo], s1_same).wait_send()


def hand_on(*refs):
    copies = [pltpu.make_async_copy(refs[n], refs[7 + n], refs[14].at[n]) for n in range(7)]
    for copy in copies:
        copy.start()
    for copy in copies:
        copy.wait()


def local(go, gate, *rest):
    args = (go, gate.T) + rest
    any_spec = pl.BlockSpec(memory_space=pl.ANY)
    smem = pl.BlockSpec(memory_space=pltpu.SMEM)
    in_specs = [pl.BlockSpec(memory_space=pltpu.HBM)] * 12
    in_specs[2] = in_specs[11] = smem
    outs = [jax.ShapeDtypeStruct((TOK, 2 * HD), BF)] * 4
    outs += [jax.ShapeDtypeStruct((TXT, 2 * HD), BF)] * 2
    outs += [jax.ShapeDtypeStruct((FEAT, 2 * HD), F32)]
    V = pltpu.VMEM
    S = pltpu.SemaphoreType.DMA
    scratch = [
        V((2 * NZ, PAIR, HD), BF),
        V((2 * NZ, 2 * TXT, HD), BF),
        V((3, 2, TOK, HD), BF),
        V((TOK, FEAT), BF),
        V((FEAT, STEPS), F32),
        V((D + FPAD - FEAT, 2 * HD), BF),
        V((PACK, HD), BF),
        V((2, NZ, PACK, HD), BF),
        V((NZ, PAIR, FPAD), BF),
        V((PAIR, HD), BF),
        V((PAIR, HD), BF),
        V((2, HD, PAIR), BF),
        V((2 * NZ, TOK, PAIR), F32),
        V((8, PAIR), F32),
        V((HD, PAIR), F32),
        V((HD, PAIR), F32),
        V((PAIR, HD), F32),
        V((PAIR, 2 * HD), F32),
        V((PAIR, HD), BF),
        V((2 * NZ, PAIR, HD), BF),
        V((2 * NZ, 2 * TXT, HD), BF),
        V((2, 2, 4, PAIR, HD), BF),
        V((2, 2, 4, 2 * TXT, HD), BF),
        V((NZ, 2, FEAT, HD), BF),
        V((2, 2, 4, FEAT, HD), BF),
        V((PAIR, HD), BF),
        V((2 * TXT, HD), BF),
        V((2, 2, TOK, HD), BF),
        V((2, TOK, HD), BF),
        S((10,)),
        S((13,)),
        S((13,)),
        S((2, 2, 4)),
        S((2, 2, 4)),
        S((2, 2, 4)),
        S((2, 2, 4)),
        S((2,)),
        S((2,)),
        S((2, 2)),
        S((2, 2)),
        S((2,)),
        S((2,)),
        S((4, 2)),
        S((4, 2)),
        S((2, 2, 4)),
        S((2, 2, 4)),
        S((2, 2, 4)),
        S((2, 2, 4)),
        S((2, 2, 4)),
        S((2, 2, 4)),
    ]
    results = pl.pallas_call(
        kernel,
        out_shape=[V(out.shape, out.dtype) for out in outs],
        in_specs=in_specs,
        out_specs=[pl.BlockSpec(memory_space=V)] * 7,
        scratch_shapes=scratch,
        compiler_params=pltpu.CompilerParams(
            collective_id=0, has_side_effects=True, vmem_limit_bytes=56 * 1024 * 1024
        ),
    )(*args)
    return pl.pallas_call(
        hand_on,
        out_shape=outs,
        in_specs=[any_spec] * 7,
        out_specs=[any_spec] * 7,
        scratch_shapes=[S((7,))],
    )(*[pltpu.with_memory_space_constraint(result, V) for result in results])


def solution(mesh):
    return jax.shard_map(
        local,
        mesh=mesh,
        in_specs=(
            P("ctx", "patch"),
            P(None, "patch"),
            P(),
            P(None, "patch"),
            P("ctx", "patch"),
            P("ctx", "patch"),
            P("ctx", "patch"),
            P("ctx", "patch"),
            P("ctx", "patch"),
            P("ctx", "patch"),
            P("ctx", "patch"),
            P(),
        ),
        out_specs=(P("ctx", "patch"),) * 7,
        check_vma=False,
    )
```

```python
import math

import jax
import jax.numpy as jnp
from jax import lax
from jax.experimental import pallas as pl
from jax.experimental.pallas import tpu as pltpu
from jax.sharding import PartitionSpec as P

HD = 128
TOK = 192
PAIR = 2 * TOK
TXT = 32
NZ = 8
FEAT = 320
FPAD = 384
PACK = 2 * TOK + TOK // 2
D = 5120
STEPS = 1000
BF = jnp.bfloat16
F32 = jnp.float32
MESH = pl.DeviceIdType.MESH
FACTOR = 1.0 / math.sqrt(HD)

NN = (((1,), (0,)), ((), ()))
NT = (((1,), (1,)), ((), ()))
TN = (((0,), (0,)), ((), ()))


def mm(a, b, dims):
    return lax.dot_general(a, b, dims, preferred_element_type=F32)


def kernel(
    go_h, gate_h, ts_s, w_h, q_h, k_h, v_h, cq_h, tk_h, tv_h, cg_h, tc_s,
    OQ, OK, OV, OC, OTK, OTV, OW,
    U, UT, QA, GO, GT, W, SL, SB, SU, GS, GR, AT, ST, STAT, OT, DQT, DO, DW, DOB, R, RT, RR, RRT, GP, GG, FR, FRT, DQ, DR,
    ld, xs, xr, ags, agr, ats, atr, s1s, s1r, s2s, s2r, s2fs, s2fr, s3s, s3r, ks, kr, ts, tr, gs, gr,
):
    c = lax.axis_index("ctx")
    p = lax.axis_index("patch")
    z, xh = c // 2, lax.rem(c, 2)
    ox = 1 - xh
    y, core, xlo = p // 4, lax.rem(p, 2), lax.rem(p // 2, 2)
    zr = lambda n: lax.rem(z + n + NZ, NZ)
    yr = lambda n: lax.rem(y + n + 4, 4)
    partner = (2 * z + ox, p)
    right = (2 * zr(1) + xh, p)
    left = (2 * zr(-1) + xh, p)
    ydev = [(c, yr(n) * 4 + xlo * 2 + core) for n in (1, -1)]
    sibling = (c, p + 1 - 2 * core)
    s1_same = (2 * z + core, y * 4 + xlo * 2 + xh)
    s1_flip = (2 * z + core, y * 4 + (1 - xlo) * 2 + xh)
    diagonal = (2 * z + ox, sibling[1])
    is_self = core == xh
    own_cols = pl.ds(pl.multiple_of(xh * HD, HD), HD)
    other_cols = pl.ds(pl.multiple_of(ox * HD, HD), HD)

    def remote(src, dst, send, recv, dev):
        return pltpu.make_async_remote_copy(
            src_ref=src, dst_ref=dst, send_sem=send, recv_sem=recv, device_id=dev, device_id_type=MESH
        )

    pending = []

    def push(src, dst, send, recv, dev):
        copy = remote(src, dst, send, recv, dev)
        copy.start()
        pending.append(copy)

    def arrive(dst, send, recv):
        remote(dst, dst, send, recv, partner).wait_recv()

    loads = []

    def load(src, dst):
        copy = pltpu.make_async_copy(src, dst, ld.at[len(loads)])
        copy.start()
        loads.append(copy)

    load(tk_h.at[:, own_cols], UT.at[c, pl.ds(0, TXT)])
    load(tv_h.at[:, own_cols], UT.at[c, pl.ds(TXT, TXT)])
    load(k_h.at[:, own_cols], U.at[c, pl.ds(0, TOK)])
    load(v_h.at[:, own_cols], U.at[c, pl.ds(TOK, TOK)])
    load(gate_h, GT)
    load(go_h, GO)
    for n, src in enumerate((q_h, cq_h, cg_h)):
        load(src.at[:, own_cols], QA.at[n, xh])

    barrier = pltpu.get_barrier_semaphore()
    for dev in [partner, right, left, sibling, s1_flip, diagonal] + ydev:
        pl.semaphore_signal(barrier, inc=1, device_id=dev, device_id_type=MESH)
    W[pl.ds(D, FPAD - FEAT), :] = jnp.zeros((FPAD - FEAT, 2 * HD), BF)
    STAT[...] = jnp.full((8, PAIR), -jnp.inf, F32)
    STAT[1:2, :] = jnp.zeros((1, PAIR), F32)
    OT[...] = jnp.zeros((HD, PAIR), F32)
    DQT[...] = jnp.zeros((HD, PAIR), F32)
    DW[...] = jnp.zeros((PAIR, 2 * HD), F32)
    pl.semaphore_wait(barrier, 8)

    def cross_x(n, src, dst):
        push(src.at[:, other_cols], dst, xs.at[n], xr.at[n], partner)


    def ag_len(stream, side):
        return 4 if stream == side else 3

    def ag_unit(stream, side, n):
        return 2 * (zr(-n) if side == 0 else zr(n)) + (xh if stream == 0 else ox)

    def ag_send(buf, ss, rs, stream, side, n):
        if n < ag_len(stream, side):
            unit = ag_unit(stream, side, n)
            at = (stream, side, n)
            push(buf.at[unit], buf.at[unit], ss.at[at], rs.at[at], right if side == 0 else left)

    def ag_step(buf, ss, rs, stream, n):
        units = []
        for side in range(2):
            if n < ag_len(stream, side):
                unit = ag_unit(stream, side, n + 1)
                arrive(buf.at[unit], ss.at[stream, side, n], rs.at[stream, side, n])
                ag_send(buf, ss, rs, stream, side, n + 1)
                units.append(unit)
        return units

    def text_step(n):
        for stream in range(2):
            ag_step(UT, ats, atr, stream, n)

    block = lambda n, b: SB.at[core, 2 * yr(n) + b]

    def own_block(b):
        for n in range(2):
            push(block(0, b), block(0, b), s2s.at[n, b], s2r.at[n, b], ydev[n])
        push(block(0, b), block(0, b), s3s.at[0, b], s3r.at[0, b], sibling)

    def scaled_own():
        @pl.when(jnp.logical_not(is_self))
        def _():
            arrive(block(0, xlo), s1s.at[0], s1r.at[xlo])

        own_block(xlo)
        arrive(block(0, 1 - xlo), s1s.at[1], s1r.at[1 - xlo])
        own_block(1 - xlo)

    def scaled_near():
        for n in range(2):
            frm = 2 * n - 1
            for b in range(2):
                arrive(block(frm, b), s2s.at[n, b], s2r.at[n, b])
                if b == n:
                    push(block(frm, b), block(frm, b), s2fs.at[n], s2fr.at[n], ydev[n])
                push(block(frm, b), block(frm, b), s3s.at[1 + n, b], s3r.at[1 + n, b], sibling)

    def scaled_far():
        for b in range(2):
            arrive(block(2, b), s2fs.at[b], s2fr.at[b])
            push(block(2, b), block(2, b), s3s.at[3, b], s3r.at[3, b], sibling)

    def stacked(index):
        return QA[index].reshape(PAIR, HD)

    def rows_of(zb, at):
        return jnp.concatenate([U[2 * zb, at : at + TOK], U[2 * zb + 1, at : at + TOK]], axis=0)

    def forward(unit):
        scores = FACTOR * mm(U[unit, 0:TOK], stacked(0), NT)
        ST[unit] = scores
        top = STAT[0:1]
        new_top = jnp.maximum(top, jnp.max(scores, axis=0, keepdims=True))
        decay = jnp.exp(top - new_top)
        probs = jnp.exp(scores - new_top)
        STAT[0:1] = new_top
        STAT[1:2] = STAT[1:2] * decay + jnp.sum(probs, axis=0, keepdims=True)
        OT[...] = OT[...] * decay + mm(U[unit, TOK:PAIR], probs.astype(BF), TN)

    def kv_step(stream, n):
        return ag_step(U, ags, agr, stream, n)

    def forward_all(units):
        for unit in units:
            forward(unit)

    def rs_len(side, unit):
        return 4 if side == unit else 3

    def rs_step(n, cur, slots, ss, rs, units=(0, 1)):
        legs = [(side, unit) for side in range(2) for unit in units]
        for side, unit in sorted(legs, key=lambda leg: n < rs_len(*leg)):
            dest = zr(n) if side == 0 else zr(-n)
            dev = right if side == 0 else left
            length = rs_len(side, unit)
            ref = cur(dest, unit)
            if n < length:
                slot = slots.at[side, unit, n]
                arrive(slot, ss.at[side, unit, n], rs.at[side, unit, n])
                ref[...] = (ref[...].astype(F32) + slot[...].astype(F32)).astype(BF)
            if 0 < n <= length:
                push(ref, slots.at[side, unit, n - 1], ss.at[side, unit, n - 1], rs.at[side, unit, n - 1], dev)

    def rs_text(n):
        rs_step(n, lambda dest, unit: RT.at[2 * dest + unit], RRT, ts, tr)

    def rs_kv(n):
        rs_step(n, lambda dest, unit: R.at[2 * dest + unit], RR, ks, kr)

    def rs_weight(stream, n):
        sides(n, weight_part(stream))
        rs_step(n, lambda dest, unit: GP.at[dest, xh if unit == 0 else ox], GG, gs, gr, (stream,))

    def weight_end(stream):
        sides(0, weight_part(stream))
        head, cols = (xh, own_cols) if stream == 0 else (ox, other_cols)
        total = GP[z, head].astype(F32)
        for side in range(2):
            arrive(GG.at[side, stream, 0], gs.at[side, stream, 0], gr.at[side, stream, 0])
            total = total + GG[side, stream, 0].astype(F32)
        OW[0:HD, cols] = total[0:HD].T
        OW[HD : 2 * HD, cols] = total[HD : 2 * HD].T
        rest = total[2 * HD :]
        OW[2 * HD :, cols] = jnp.concatenate([rest[:, : HD // 2], rest[:, HD // 2 :]], axis=0).T

    def text():
        tkeys = UT[:, 0:TXT, :].reshape(2 * NZ * TXT, HD)
        tvalues = UT[:, TXT:, :].reshape(2 * NZ * TXT, HD)
        cgrad, cquery = stacked(2), stacked(1)
        tscores = FACTOR * mm(tkeys, cquery, NT)
        live = lax.broadcasted_iota(jnp.int32, (2 * NZ * TXT, 1), 0) < tc_s[0]
        tscores = jnp.where(live, tscores, -jnp.inf)
        ttop = jnp.max(tscores, axis=0, keepdims=True)
        tmass = ttop + jnp.log(jnp.sum(jnp.exp(tscores - ttop), axis=0, keepdims=True))
        tprobs = jnp.exp(tscores - tmass).astype(BF)
        tgrad_probs = mm(tvalues, cgrad, NT)
        tdelta = jnp.sum(cgrad.astype(F32).T * mm(tvalues, tprobs, TN), axis=0, keepdims=True)
        tgrad_scores = (tprobs.astype(F32) * (tgrad_probs - tdelta)).astype(BF)
        RT[:, 0:TXT, :] = (FACTOR * mm(tgrad_scores, cquery, NN)).astype(BF).reshape(2 * NZ, TXT, HD)
        RT[:, TXT:, :] = mm(tprobs, cgrad, NN).astype(BF).reshape(2 * NZ, TXT, HD)
        dcross = FACTOR * mm(tkeys, tgrad_scores, TN)
        DQ[1] = dcross.T.astype(BF).reshape(2, TOK, HD)
        push(DQ.at[1, ox], DR.at[1], xs.at[11], xr.at[11], partner)

    def project_part(frm, n):
        for b in range(2):
            arrive(SB.at[1 - core, 2 * yr(frm) + b], s3s.at[n, b], s3r.at[n, b])

        def part(b, carry):
            j = 2 * yr(frm) + b
            rows = []
            for s in range(2):
                rest = SB[s, j, PAIR:PACK]
                rest = jnp.concatenate([rest[:, : HD // 2], rest[:, HD // 2 :]], axis=0)
                rows.append(
                    jnp.concatenate([SB[s, j, 0:TOK], SB[s, j, TOK:PAIR], rest, jnp.zeros((TOK, HD // 2), BF)], axis=1)
                )
            rows = jnp.concatenate(rows, axis=0)
            SU[j] = rows
            weight = W[pl.ds(pl.multiple_of(FEAT * (2 * j + xh), 64), FPAD), :]
            DW[...] = DW[...] + mm(rows, weight, NN)
            return carry

        lax.fori_loop(0, 2, part, 0)

    def project_end():
        low, high = DW[:, :HD], DW[:, HD:]
        mine = xh == 0
        GS[...] = jnp.where(mine, high, low).astype(BF)
        push(GS, GR, xs.at[7], xr.at[7], partner)
        DO[...] = jnp.where(mine, low, high)

    def backward(zb):
        keys, vals = rows_of(zb, 0), rows_of(zb, TOK)
        out_grad = DOB[...]
        scores = ST[pl.ds(2 * zb, 2)].reshape(PAIR, PAIR)
        probs = jnp.exp(scores - STAT[2:3]).astype(BF)
        grad_scores = (probs.astype(F32) * (mm(vals, out_grad, NT) - STAT[3:4])).astype(BF)
        dvals = mm(probs, out_grad, NN).astype(BF)
        dkeys = (FACTOR * mm(grad_scores, stacked(0), NN)).astype(BF)
        DQT[...] = DQT[...] + mm(keys, grad_scores, TN)
        for s in range(2):
            R[2 * zb + s, 0:TOK] = dkeys[s * TOK : (s + 1) * TOK]
            R[2 * zb + s, TOK:PAIR] = dvals[s * TOK : (s + 1) * TOK]

    def weight_part(stream):
        head = xh if stream == 0 else ox

        def one(j):
            part = mm(AT[head], SU[j], NN).astype(BF)
            GP[j, head, 0:HD] = part[:, 0:HD]
            GP[j, head, HD : 2 * HD] = part[:, HD : 2 * HD]
            GP[j, head, 2 * HD :] = jnp.concatenate([part[: HD // 2, 2 * HD : FEAT], part[HD // 2 :, 2 * HD : FEAT]], axis=1)

        return one

    def sides(n, step):
        if n in (0, 4):
            step(zr(n))
        else:

            def one(side, carry):
                step(zr((1 - 2 * side) * n))
                return carry

            lax.fori_loop(0, 2, one, 0)

    cross_x(0, tk_h, UT.at[c, pl.ds(0, TXT)])
    cross_x(1, tv_h, UT.at[c, pl.ds(TXT, TXT)])
    cross_x(2, k_h, U.at[c, pl.ds(0, TOK)])
    cross_x(3, v_h, U.at[c, pl.ds(TOK, TOK)])
    cross_x(4, q_h, QA.at[0, xh])
    loads[0].wait()
    loads[1].wait()
    for side in range(2):
        ag_send(UT, ats, atr, 0, side, 0)
    loads[2].wait()
    loads[3].wait()
    for side in range(2):
        ag_send(U, ags, agr, 0, side, 0)

    loads[4].wait()
    loads[5].wait()
    chosen = lax.broadcasted_iota(jnp.int32, (1, STEPS), 1) == ts_s[0]
    gate_col = jnp.sum(jnp.where(chosen, GT[...], 0.0), axis=1, keepdims=True)
    gate_row = jnp.broadcast_to(gate_col, (FEAT, HD)).T[0:1]
    scaled = (gate_row * GO[...].astype(F32)).astype(BF)
    SL[0:TOK] = scaled[:, :HD]
    SL[TOK:PAIR] = scaled[:, HD : 2 * HD]
    SL[PAIR:PACK] = jnp.concatenate([scaled[: TOK // 2, 2 * HD :], scaled[TOK // 2 :, 2 * HD :]], axis=1)
    j0 = 2 * y + xlo
    push(SL, SB.at[xh, j0], s1s.at[1], s1r.at[xlo], s1_flip)

    @pl.when(is_self)
    def _():
        SB[xh, j0] = SL[...]

    @pl.when(jnp.logical_not(is_self))
    def _():
        remote(SL, SB.at[xh, j0], s1s.at[0], s1r.at[xlo], s1_same).start()

    load(w_h, W.at[pl.ds(0, D)])

    arrive(UT.at[2 * z + ox, pl.ds(0, TXT)], xs.at[0], xr.at[0])
    arrive(UT.at[2 * z + ox, pl.ds(TXT, TXT)], xs.at[1], xr.at[1])
    for side in range(2):
        ag_send(UT, ats, atr, 1, side, 0)
    for n in range(2):
        arrive(U.at[2 * z + ox, pl.ds(n * TOK, TOK)], xs.at[2 + n], xr.at[2 + n])
    for side in range(2):
        ag_send(U, ags, agr, 1, side, 0)

    a0 = kv_step(0, 0)
    scaled_own()
    cross_x(5, cq_h, QA.at[1, xh])
    cross_x(6, cg_h, QA.at[2, xh])
    b0 = kv_step(1, 0)
    loads[6].wait()
    arrive(QA.at[0, ox], xs.at[4], xr.at[4])
    a1 = kv_step(0, 1)
    forward_all([c, 2 * z + ox] + a0 + b0 + a1)
    text_step(0)
    b1 = kv_step(1, 1)
    scaled_near()
    forward_all(b1)
    a2 = kv_step(0, 2)
    text_step(1)
    scaled_far()
    b2 = kv_step(1, 2)
    forward_all(a2 + b2)
    text_step(2)
    loads[9].wait()
    project_part(0, 0)
    project_part(-1, 1)
    project_part(1, 2)
    project_part(2, 3)
    project_end()
    a3 = kv_step(0, 3)
    forward_all(a3)
    text_step(3)
    b3 = kv_step(1, 3)
    forward_all(b3)
    mass = STAT[1:2]
    OT[...] = OT[...] / mass
    AT[xh] = OT[...].astype(BF)
    push(AT.at[xh], AT.at[xh], xs.at[8], xr.at[8], partner)
    STAT[2:3] = STAT[0:1] + jnp.log(mass)
    arrive(GR, xs.at[7], xr.at[7])
    DO[...] = DO[...] + GR[...].astype(F32)
    DOB[...] = DO[...].astype(BF)
    STAT[3:4] = jnp.sum(DOB[...].astype(F32).T * OT[...], axis=0, keepdims=True)
    backward(zr(4))
    rs_kv(4)
    rs_weight(0, 4)
    arrive(AT.at[ox], xs.at[8], xr.at[8])
    rs_weight(1, 4)
    sides(3, backward)
    loads[7].wait()
    loads[8].wait()
    arrive(QA.at[1, ox], xs.at[5], xr.at[5])
    arrive(QA.at[2, ox], xs.at[6], xr.at[6])
    text()
    rs_text(4)
    rs_kv(3)
    rs_weight(0, 3)
    rs_weight(1, 3)
    rs_text(3)
    sides(2, backward)
    backward(z)
    rs_kv(2)
    rs_weight(0, 2)
    rs_weight(1, 2)
    rs_text(2)
    sides(1, backward)
    DQ[0] = (FACTOR * DQT[...]).T.astype(BF).reshape(2, TOK, HD)
    push(DQ.at[0, ox], DR.at[0], xs.at[12], xr.at[12], partner)
    rs_kv(1)
    rs_text(1)
    rs_weight(0, 1)
    rs_weight(1, 1)
    rs_kv(0)
    push(R.at[2 * z + ox], FR, xs.at[10], xr.at[10], partner)
    rs_text(0)
    push(RT.at[2 * z + ox], FRT, xs.at[9], xr.at[9], partner)
    weight_end(0)
    weight_end(1)

    arrive(FRT, xs.at[9], xr.at[9])
    arrive(FR, xs.at[10], xr.at[10])
    arrive(DR.at[1], xs.at[11], xr.at[11])
    arrive(DR.at[0], xs.at[12], xr.at[12])
    for ref, mine, other, at, rows in (
        (OK, R, FR, 0, TOK),
        (OV, R, FR, TOK, TOK),
        (OTK, RT, FRT, 0, TXT),
        (OTV, RT, FRT, TXT, TXT),
    ):
        ref[:, own_cols] = mine[c, at : at + rows]
        ref[:, other_cols] = other[at : at + rows]
    for n, ref in enumerate((OQ, OC)):
        ref[:, own_cols] = DQ[n, xh]
        ref[:, other_cols] = DR[n]
    for copy in pending:
        copy.wait_send()

    @pl.when(jnp.logical_not(is_self))
    def _():
        remote(SL, SB.at[xh, j0], s1s.at[0], s1r.at[xlo], s1_same).wait_send()


def hand_on(*refs):
    copies = [pltpu.make_async_copy(refs[n], refs[7 + n], refs[14].at[n]) for n in range(7)]
    for copy in copies:
        copy.start()
    for copy in copies:
        copy.wait()


def local(go, gate, *rest):
    args = (go, gate.T) + rest
    any_spec = pl.BlockSpec(memory_space=pl.ANY)
    smem = pl.BlockSpec(memory_space=pltpu.SMEM)
    in_specs = [pl.BlockSpec(memory_space=pltpu.HBM)] * 12
    in_specs[2] = in_specs[11] = smem
    outs = [jax.ShapeDtypeStruct((TOK, 2 * HD), BF)] * 4
    outs += [jax.ShapeDtypeStruct((TXT, 2 * HD), BF)] * 2
    outs += [jax.ShapeDtypeStruct((FEAT, 2 * HD), F32)]
    V = pltpu.VMEM
    S = pltpu.SemaphoreType.DMA
    scratch = [
        V((2 * NZ, PAIR, HD), BF),
        V((2 * NZ, 2 * TXT, HD), BF),
        V((3, 2, TOK, HD), BF),
        V((TOK, FEAT), BF),
        V((FEAT, STEPS), F32),
        V((D + FPAD - FEAT, 2 * HD), BF),
        V((PACK, HD), BF),
        V((2, NZ, PACK, HD), BF),
        V((NZ, PAIR, FPAD), BF),
        V((PAIR, HD), BF),
        V((PAIR, HD), BF),
        V((2, HD, PAIR), BF),
        V((2 * NZ, TOK, PAIR), F32),
        V((8, PAIR), F32),
        V((HD, PAIR), F32),
        V((HD, PAIR), F32),
        V((PAIR, HD), F32),
        V((PAIR, 2 * HD), F32),
        V((PAIR, HD), BF),
        V((2 * NZ, PAIR, HD), BF),
        V((2 * NZ, 2 * TXT, HD), BF),
        V((2, 2, 4, PAIR, HD), BF),
        V((2, 2, 4, 2 * TXT, HD), BF),
        V((NZ, 2, FEAT, HD), BF),
        V((2, 2, 4, FEAT, HD), BF),
        V((PAIR, HD), BF),
        V((2 * TXT, HD), BF),
        V((2, 2, TOK, HD), BF),
        V((2, TOK, HD), BF),
        S((10,)),
        S((13,)),
        S((13,)),
        S((2, 2, 4)),
        S((2, 2, 4)),
        S((2, 2, 4)),
        S((2, 2, 4)),
        S((2,)),
        S((2,)),
        S((2, 2)),
        S((2, 2)),
        S((2,)),
        S((2,)),
        S((4, 2)),
        S((4, 2)),
        S((2, 2, 4)),
        S((2, 2, 4)),
        S((2, 2, 4)),
        S((2, 2, 4)),
        S((2, 2, 4)),
        S((2, 2, 4)),
    ]
    results = pl.pallas_call(
        kernel,
        out_shape=[V(out.shape, out.dtype) for out in outs],
        in_specs=in_specs,
        out_specs=[pl.BlockSpec(memory_space=V)] * 7,
        scratch_shapes=scratch,
        compiler_params=pltpu.CompilerParams(
            collective_id=0, has_side_effects=True, vmem_limit_bytes=56 * 1024 * 1024
        ),
    )(*args)
    return pl.pallas_call(
        hand_on,
        out_shape=outs,
        in_specs=[any_spec] * 7,
        out_specs=[any_spec] * 7,
        scratch_shapes=[S((7,))],
    )(*[pltpu.with_memory_space_constraint(result, V) for result in results])


def solution(mesh):
    return jax.shard_map(
        local,
        mesh=mesh,
        in_specs=(
            P("ctx", "patch"),
            P(None, "patch"),
            P(),
            P(None, "patch"),
            P("ctx", "patch"),
            P("ctx", "patch"),
            P("ctx", "patch"),
            P("ctx", "patch"),
            P("ctx", "patch"),
            P("ctx", "patch"),
            P("ctx", "patch"),
            P(),
        ),
        out_specs=(P("ctx", "patch"),) * 7,
        check_vma=False,
    )
```

```python
import math

import jax
import jax.numpy as jnp
from jax import lax
from jax.experimental import pallas as pl
from jax.experimental.pallas import tpu as pltpu
from jax.sharding import PartitionSpec as P

HD = 128
TOK = 192
PAIR = 2 * TOK
TXT = 32
NZ = 8
FEAT = 320
FPAD = 384
PACK = 2 * TOK + TOK // 2
D = 5120
STEPS = 1000
BF = jnp.bfloat16
F32 = jnp.float32
MESH = pl.DeviceIdType.MESH
FACTOR = 1.0 / math.sqrt(HD)

NN = (((1,), (0,)), ((), ()))
NT = (((1,), (1,)), ((), ()))
TN = (((0,), (0,)), ((), ()))


def mm(a, b, dims):
    return lax.dot_general(a, b, dims, preferred_element_type=F32)


def kernel(
    go_h, gate_h, ts_s, w_h, q_h, k_h, v_h, cq_h, tk_h, tv_h, cg_h, tc_s,
    OQ, OK, OV, OC, OTK, OTV, OW,
    U, UT, QA, GO, GT, W, SL, SB, SU, GS, GR, AT, ST, STAT, OT, DQT, DO, DW, DOB, R, RT, RR, RRT, GP, GG, FR, FRT, DQ, DR,
    ld, xs, xr, ags, agr, ats, atr, s1s, s1r, s2s, s2r, s2fs, s2fr, s3s, s3r, ks, kr, ts, tr, gs, gr,
):
    c = lax.axis_index("ctx")
    p = lax.axis_index("patch")
    z, xh = c // 2, lax.rem(c, 2)
    ox = 1 - xh
    y, core, xlo = p // 4, lax.rem(p, 2), lax.rem(p // 2, 2)
    zr = lambda n: lax.rem(z + n + NZ, NZ)
    yr = lambda n: lax.rem(y + n + 4, 4)
    partner = (2 * z + ox, p)
    right = (2 * zr(1) + xh, p)
    left = (2 * zr(-1) + xh, p)
    ydev = [(c, yr(n) * 4 + xlo * 2 + core) for n in (1, -1)]
    sibling = (c, p + 1 - 2 * core)
    s1_same = (2 * z + core, y * 4 + xlo * 2 + xh)
    s1_flip = (2 * z + core, y * 4 + (1 - xlo) * 2 + xh)
    diagonal = (2 * z + ox, sibling[1])
    is_self = core == xh
    own_cols = pl.ds(pl.multiple_of(xh * HD, HD), HD)
    other_cols = pl.ds(pl.multiple_of(ox * HD, HD), HD)

    def remote(src, dst, send, recv, dev):
        return pltpu.make_async_remote_copy(
            src_ref=src, dst_ref=dst, send_sem=send, recv_sem=recv, device_id=dev, device_id_type=MESH
        )

    pending = []

    def push(src, dst, send, recv, dev):
        copy = remote(src, dst, send, recv, dev)
        copy.start()
        pending.append(copy)

    def arrive(dst, send, recv):
        remote(dst, dst, send, recv, partner).wait_recv()

    loads = []

    def load(src, dst):
        copy = pltpu.make_async_copy(src, dst, ld.at[len(loads)])
        copy.start()
        loads.append(copy)

    load(tk_h.at[:, own_cols], UT.at[c, pl.ds(0, TXT)])
    load(tv_h.at[:, own_cols], UT.at[c, pl.ds(TXT, TXT)])
    load(k_h.at[:, own_cols], U.at[c, pl.ds(0, TOK)])
    load(v_h.at[:, own_cols], U.at[c, pl.ds(TOK, TOK)])
    load(gate_h, GT)
    load(go_h, GO)
    for n, src in enumerate((q_h, cq_h, cg_h)):
        load(src.at[:, own_cols], QA.at[n, xh])

    barrier = pltpu.get_barrier_semaphore()
    for dev in [partner, right, left, sibling, s1_flip, diagonal] + ydev:
        pl.semaphore_signal(barrier, inc=1, device_id=dev, device_id_type=MESH)
    W[pl.ds(D, FPAD - FEAT), :] = jnp.zeros((FPAD - FEAT, 2 * HD), BF)
    STAT[...] = jnp.full((8, PAIR), -jnp.inf, F32)
    STAT[1:2, :] = jnp.zeros((1, PAIR), F32)
    OT[...] = jnp.zeros((HD, PAIR), F32)
    DQT[...] = jnp.zeros((HD, PAIR), F32)
    DW[...] = jnp.zeros((PAIR, 2 * HD), F32)
    pl.semaphore_wait(barrier, 8)

    def cross_x(n, src, dst):
        push(src.at[:, other_cols], dst, xs.at[n], xr.at[n], partner)


    def ag_len(stream, side):
        return 4 if stream == side else 3

    def ag_unit(stream, side, n):
        return 2 * (zr(-n) if side == 0 else zr(n)) + (xh if stream == 0 else ox)

    def ag_send(buf, ss, rs, stream, side, n):
        if n < ag_len(stream, side):
            unit = ag_unit(stream, side, n)
            at = (stream, side, n)
            push(buf.at[unit], buf.at[unit], ss.at[at], rs.at[at], right if side == 0 else left)

    def ag_step(buf, ss, rs, stream, n):
        units = []
        for side in range(2):
            if n < ag_len(stream, side):
                unit = ag_unit(stream, side, n + 1)
                arrive(buf.at[unit], ss.at[stream, side, n], rs.at[stream, side, n])
                ag_send(buf, ss, rs, stream, side, n + 1)
                units.append(unit)
        return units

    def text_step(n):
        for stream in range(2):
            ag_step(UT, ats, atr, stream, n)

    block = lambda n, b: SB.at[core, 2 * yr(n) + b]

    def own_block(b):
        for n in range(2):
            push(block(0, b), block(0, b), s2s.at[n, b], s2r.at[n, b], ydev[n])
        push(block(0, b), block(0, b), s3s.at[0, b], s3r.at[0, b], sibling)

    def scaled_own():
        @pl.when(jnp.logical_not(is_self))
        def _():
            arrive(block(0, xlo), s1s.at[0], s1r.at[xlo])

        own_block(xlo)
        arrive(block(0, 1 - xlo), s1s.at[1], s1r.at[1 - xlo])
        own_block(1 - xlo)

    def scaled_near():
        for n in range(2):
            frm = 2 * n - 1
            for b in range(2):
                arrive(block(frm, b), s2s.at[n, b], s2r.at[n, b])
                if b == n:
                    push(block(frm, b), block(frm, b), s2fs.at[n], s2fr.at[n], ydev[n])
                push(block(frm, b), block(frm, b), s3s.at[1 + n, b], s3r.at[1 + n, b], sibling)

    def scaled_far():
        for b in range(2):
            arrive(block(2, b), s2fs.at[b], s2fr.at[b])
            push(block(2, b), block(2, b), s3s.at[3, b], s3r.at[3, b], sibling)

    def stacked(index):
        return QA[index].reshape(PAIR, HD)

    def rows_of(zb, at):
        return jnp.concatenate([U[2 * zb, at : at + TOK], U[2 * zb + 1, at : at + TOK]], axis=0)

    def forward(unit):
        scores = FACTOR * mm(U[unit, 0:TOK], stacked(0), NT)
        ST[unit] = scores
        top = STAT[0:1]
        new_top = jnp.maximum(top, jnp.max(scores, axis=0, keepdims=True))
        decay = jnp.exp(top - new_top)
        probs = jnp.exp(scores - new_top)
        STAT[0:1] = new_top
        STAT[1:2] = STAT[1:2] * decay + jnp.sum(probs, axis=0, keepdims=True)
        OT[...] = OT[...] * decay + mm(U[unit, TOK:PAIR], probs.astype(BF), TN)

    def kv_step(stream, n):
        return ag_step(U, ags, agr, stream, n)

    def forward_all(units):
        for unit in units:
            forward(unit)

    def rs_len(side, unit):
        return 4 if side == unit else 3

    def rs_step(n, cur, slots, ss, rs, units=(0, 1), only=None):
        legs = [(side, unit) for side in range(2) for unit in units]
        if only is not None:
            legs = [leg for leg in legs if (n < rs_len(*leg)) == (only == 1)]
        for side, unit in sorted(legs, key=lambda leg: n < rs_len(*leg)):
            dest = zr(n) if side == 0 else zr(-n)
            dev = right if side == 0 else left
            length = rs_len(side, unit)
            ref = cur(dest, unit)
            if n < length:
                slot = slots.at[side, unit, n]
                arrive(slot, ss.at[side, unit, n], rs.at[side, unit, n])
                ref[...] = (ref[...].astype(F32) + slot[...].astype(F32)).astype(BF)
            if 0 < n <= length:
                push(ref, slots.at[side, unit, n - 1], ss.at[side, unit, n - 1], rs.at[side, unit, n - 1], dev)

    def rs_text(n):
        rs_step(n, lambda dest, unit: RT.at[2 * dest + unit], RRT, ts, tr)

    def rs_kv(n, only=None):
        rs_step(n, lambda dest, unit: R.at[2 * dest + unit], RR, ks, kr, only=only)

    def rs_weight(stream, n):
        sides(n, weight_part(stream))
        rs_step(n, lambda dest, unit: GP.at[dest, xh if unit == 0 else ox], GG, gs, gr, (stream,))

    def weight_end(stream):
        sides(0, weight_part(stream))
        head, cols = (xh, own_cols) if stream == 0 else (ox, other_cols)
        total = GP[z, head].astype(F32)
        for side in range(2):
            arrive(GG.at[side, stream, 0], gs.at[side, stream, 0], gr.at[side, stream, 0])
            total = total + GG[side, stream, 0].astype(F32)
        OW[0:HD, cols] = total[0:HD].T
        OW[HD : 2 * HD, cols] = total[HD : 2 * HD].T
        rest = total[2 * HD :]
        OW[2 * HD :, cols] = jnp.concatenate([rest[:, : HD // 2], rest[:, HD // 2 :]], axis=0).T

    def text():
        tkeys = UT[:, 0:TXT, :].reshape(2 * NZ * TXT, HD)
        tvalues = UT[:, TXT:, :].reshape(2 * NZ * TXT, HD)
        cgrad, cquery = stacked(2), stacked(1)
        tscores = FACTOR * mm(tkeys, cquery, NT)
        live = lax.broadcasted_iota(jnp.int32, (2 * NZ * TXT, 1), 0) < tc_s[0]
        tscores = jnp.where(live, tscores, -jnp.inf)
        ttop = jnp.max(tscores, axis=0, keepdims=True)
        tmass = ttop + jnp.log(jnp.sum(jnp.exp(tscores - ttop), axis=0, keepdims=True))
        tprobs = jnp.exp(tscores - tmass).astype(BF)
        tgrad_probs = mm(tvalues, cgrad, NT)
        tdelta = jnp.sum(cgrad.astype(F32).T * mm(tvalues, tprobs, TN), axis=0, keepdims=True)
        tgrad_scores = (tprobs.astype(F32) * (tgrad_probs - tdelta)).astype(BF)
        RT[:, 0:TXT, :] = (FACTOR * mm(tgrad_scores, cquery, NN)).astype(BF).reshape(2 * NZ, TXT, HD)
        RT[:, TXT:, :] = mm(tprobs, cgrad, NN).astype(BF).reshape(2 * NZ, TXT, HD)
        dcross = FACTOR * mm(tkeys, tgrad_scores, TN)
        DQ[1] = dcross.T.astype(BF).reshape(2, TOK, HD)
        push(DQ.at[1, ox], DR.at[1], xs.at[11], xr.at[11], partner)

    def project_part(frm, n):
        for b in range(2):
            arrive(SB.at[1 - core, 2 * yr(frm) + b], s3s.at[n, b], s3r.at[n, b])

        def part(b, carry):
            j = 2 * yr(frm) + b
            rows = []
            for s in range(2):
                rest = SB[s, j, PAIR:PACK]
                rest = jnp.concatenate([rest[:, : HD // 2], rest[:, HD // 2 :]], axis=0)
                rows.append(
                    jnp.concatenate([SB[s, j, 0:TOK], SB[s, j, TOK:PAIR], rest, jnp.zeros((TOK, HD // 2), BF)], axis=1)
                )
            rows = jnp.concatenate(rows, axis=0)
            SU[j] = rows
            weight = W[pl.ds(pl.multiple_of(FEAT * (2 * j + xh), 64), FPAD), :]
            DW[...] = DW[...] + mm(rows, weight, NN)
            return carry

        lax.fori_loop(0, 2, part, 0)

    def project_end():
        low, high = DW[:, :HD], DW[:, HD:]
        mine = xh == 0
        GS[...] = jnp.where(mine, high, low).astype(BF)
        push(GS, GR, xs.at[7], xr.at[7], partner)
        DO[...] = jnp.where(mine, low, high)

    def backward(zb):
        keys, vals = rows_of(zb, 0), rows_of(zb, TOK)
        out_grad = DOB[...]
        scores = ST[pl.ds(2 * zb, 2)].reshape(PAIR, PAIR)
        probs = jnp.exp(scores - STAT[2:3]).astype(BF)
        grad_scores = (probs.astype(F32) * (mm(vals, out_grad, NT) - STAT[3:4])).astype(BF)
        dvals = mm(probs, out_grad, NN).astype(BF)
        dkeys = (FACTOR * mm(grad_scores, stacked(0), NN)).astype(BF)
        DQT[...] = DQT[...] + mm(keys, grad_scores, TN)
        for s in range(2):
            R[2 * zb + s, 0:TOK] = dkeys[s * TOK : (s + 1) * TOK]
            R[2 * zb + s, TOK:PAIR] = dvals[s * TOK : (s + 1) * TOK]

    def weight_part(stream):
        head = xh if stream == 0 else ox

        def one(j):
            part = mm(AT[head], SU[j], NN).astype(BF)
            GP[j, head, 0:HD] = part[:, 0:HD]
            GP[j, head, HD : 2 * HD] = part[:, HD : 2 * HD]
            GP[j, head, 2 * HD :] = jnp.concatenate([part[: HD // 2, 2 * HD : FEAT], part[HD // 2 :, 2 * HD : FEAT]], axis=1)

        return one

    def sides(n, step):
        if n in (0, 4):
            step(zr(n))
        else:

            def one(side, carry):
                step(zr((1 - 2 * side) * n))
                return carry

            lax.fori_loop(0, 2, one, 0)

    cross_x(0, tk_h, UT.at[c, pl.ds(0, TXT)])
    cross_x(1, tv_h, UT.at[c, pl.ds(TXT, TXT)])
    cross_x(2, k_h, U.at[c, pl.ds(0, TOK)])
    cross_x(3, v_h, U.at[c, pl.ds(TOK, TOK)])
    cross_x(4, q_h, QA.at[0, xh])
    loads[0].wait()
    loads[1].wait()
    for side in range(2):
        ag_send(UT, ats, atr, 0, side, 0)
    loads[2].wait()
    loads[3].wait()
    for side in range(2):
        ag_send(U, ags, agr, 0, side, 0)

    loads[4].wait()
    loads[5].wait()
    chosen = lax.broadcasted_iota(jnp.int32, (1, STEPS), 1) == ts_s[0]
    gate_col = jnp.sum(jnp.where(chosen, GT[...], 0.0), axis=1, keepdims=True)
    gate_row = jnp.broadcast_to(gate_col, (FEAT, HD)).T[0:1]
    scaled = (gate_row * GO[...].astype(F32)).astype(BF)
    SL[0:TOK] = scaled[:, :HD]
    SL[TOK:PAIR] = scaled[:, HD : 2 * HD]
    SL[PAIR:PACK] = jnp.concatenate([scaled[: TOK // 2, 2 * HD :], scaled[TOK // 2 :, 2 * HD :]], axis=1)
    j0 = 2 * y + xlo
    push(SL, SB.at[xh, j0], s1s.at[1], s1r.at[xlo], s1_flip)

    @pl.when(is_self)
    def _():
        SB[xh, j0] = SL[...]

    @pl.when(jnp.logical_not(is_self))
    def _():
        remote(SL, SB.at[xh, j0], s1s.at[0], s1r.at[xlo], s1_same).start()

    load(w_h, W.at[pl.ds(0, D)])

    arrive(UT.at[2 * z + ox, pl.ds(0, TXT)], xs.at[0], xr.at[0])
    arrive(UT.at[2 * z + ox, pl.ds(TXT, TXT)], xs.at[1], xr.at[1])
    for side in range(2):
        ag_send(UT, ats, atr, 1, side, 0)
    for n in range(2):
        arrive(U.at[2 * z + ox, pl.ds(n * TOK, TOK)], xs.at[2 + n], xr.at[2 + n])
    for side in range(2):
        ag_send(U, ags, agr, 1, side, 0)

    a0 = kv_step(0, 0)
    scaled_own()
    cross_x(5, cq_h, QA.at[1, xh])
    cross_x(6, cg_h, QA.at[2, xh])
    b0 = kv_step(1, 0)
    loads[6].wait()
    arrive(QA.at[0, ox], xs.at[4], xr.at[4])
    a1 = kv_step(0, 1)
    forward_all([c, 2 * z + ox] + a0 + b0 + a1)
    text_step(0)
    b1 = kv_step(1, 1)
    scaled_near()
    forward_all(b1)
    a2 = kv_step(0, 2)
    text_step(1)
    scaled_far()
    b2 = kv_step(1, 2)
    forward_all(a2 + b2)
    text_step(2)
    loads[9].wait()
    project_part(0, 0)
    project_part(-1, 1)
    project_part(1, 2)
    project_part(2, 3)
    project_end()
    a3 = kv_step(0, 3)
    forward_all(a3)
    text_step(3)
    b3 = kv_step(1, 3)
    forward_all(b3)
    mass = STAT[1:2]
    OT[...] = OT[...] / mass
    AT[xh] = OT[...].astype(BF)
    push(AT.at[xh], AT.at[xh], xs.at[8], xr.at[8], partner)
    STAT[2:3] = STAT[0:1] + jnp.log(mass)
    arrive(GR, xs.at[7], xr.at[7])
    DO[...] = DO[...] + GR[...].astype(F32)
    DOB[...] = DO[...].astype(BF)
    STAT[3:4] = jnp.sum(DOB[...].astype(F32).T * OT[...], axis=0, keepdims=True)
    backward(zr(4))
    rs_kv(4)
    rs_weight(0, 4)
    arrive(AT.at[ox], xs.at[8], xr.at[8])
    rs_weight(1, 4)
    sides(3, backward)
    rs_kv(3, 0)
    loads[7].wait()
    loads[8].wait()
    arrive(QA.at[1, ox], xs.at[5], xr.at[5])
    arrive(QA.at[2, ox], xs.at[6], xr.at[6])
    text()
    rs_text(4)
    rs_kv(3, 1)
    rs_weight(0, 3)
    rs_weight(1, 3)
    rs_text(3)
    sides(2, backward)
    backward(z)
    rs_kv(2)
    rs_weight(0, 2)
    rs_weight(1, 2)
    rs_text(2)
    sides(1, backward)
    DQ[0] = (FACTOR * DQT[...]).T.astype(BF).reshape(2, TOK, HD)
    push(DQ.at[0, ox], DR.at[0], xs.at[12], xr.at[12], partner)
    rs_kv(1)
    rs_text(1)
    rs_weight(0, 1)
    rs_weight(1, 1)
    rs_kv(0)
    push(R.at[2 * z + ox], FR, xs.at[10], xr.at[10], partner)
    rs_text(0)
    push(RT.at[2 * z + ox], FRT, xs.at[9], xr.at[9], partner)
    weight_end(0)
    weight_end(1)

    arrive(FRT, xs.at[9], xr.at[9])
    arrive(FR, xs.at[10], xr.at[10])
    arrive(DR.at[1], xs.at[11], xr.at[11])
    arrive(DR.at[0], xs.at[12], xr.at[12])
    for ref, mine, other, at, rows in (
        (OK, R, FR, 0, TOK),
        (OV, R, FR, TOK, TOK),
        (OTK, RT, FRT, 0, TXT),
        (OTV, RT, FRT, TXT, TXT),
    ):
        ref[:, own_cols] = mine[c, at : at + rows]
        ref[:, other_cols] = other[at : at + rows]
    for n, ref in enumerate((OQ, OC)):
        ref[:, own_cols] = DQ[n, xh]
        ref[:, other_cols] = DR[n]
    for copy in pending:
        copy.wait_send()

    @pl.when(jnp.logical_not(is_self))
    def _():
        remote(SL, SB.at[xh, j0], s1s.at[0], s1r.at[xlo], s1_same).wait_send()


def hand_on(*refs):
    copies = [pltpu.make_async_copy(refs[n], refs[7 + n], refs[14].at[n]) for n in range(7)]
    for copy in copies:
        copy.start()
    for copy in copies:
        copy.wait()


def local(go, gate, *rest):
    args = (go, gate.T) + rest
    any_spec = pl.BlockSpec(memory_space=pl.ANY)
    smem = pl.BlockSpec(memory_space=pltpu.SMEM)
    in_specs = [pl.BlockSpec(memory_space=pltpu.HBM)] * 12
    in_specs[2] = in_specs[11] = smem
    outs = [jax.ShapeDtypeStruct((TOK, 2 * HD), BF)] * 4
    outs += [jax.ShapeDtypeStruct((TXT, 2 * HD), BF)] * 2
    outs += [jax.ShapeDtypeStruct((FEAT, 2 * HD), F32)]
    V = pltpu.VMEM
    S = pltpu.SemaphoreType.DMA
    scratch = [
        V((2 * NZ, PAIR, HD), BF),
        V((2 * NZ, 2 * TXT, HD), BF),
        V((3, 2, TOK, HD), BF),
        V((TOK, FEAT), BF),
        V((FEAT, STEPS), F32),
        V((D + FPAD - FEAT, 2 * HD), BF),
        V((PACK, HD), BF),
        V((2, NZ, PACK, HD), BF),
        V((NZ, PAIR, FPAD), BF),
        V((PAIR, HD), BF),
        V((PAIR, HD), BF),
        V((2, HD, PAIR), BF),
        V((2 * NZ, TOK, PAIR), F32),
        V((8, PAIR), F32),
        V((HD, PAIR), F32),
        V((HD, PAIR), F32),
        V((PAIR, HD), F32),
        V((PAIR, 2 * HD), F32),
        V((PAIR, HD), BF),
        V((2 * NZ, PAIR, HD), BF),
        V((2 * NZ, 2 * TXT, HD), BF),
        V((2, 2, 4, PAIR, HD), BF),
        V((2, 2, 4, 2 * TXT, HD), BF),
        V((NZ, 2, FEAT, HD), BF),
        V((2, 2, 4, FEAT, HD), BF),
        V((PAIR, HD), BF),
        V((2 * TXT, HD), BF),
        V((2, 2, TOK, HD), BF),
        V((2, TOK, HD), BF),
        S((10,)),
        S((13,)),
        S((13,)),
        S((2, 2, 4)),
        S((2, 2, 4)),
        S((2, 2, 4)),
        S((2, 2, 4)),
        S((2,)),
        S((2,)),
        S((2, 2)),
        S((2, 2)),
        S((2,)),
        S((2,)),
        S((4, 2)),
        S((4, 2)),
        S((2, 2, 4)),
        S((2, 2, 4)),
        S((2, 2, 4)),
        S((2, 2, 4)),
        S((2, 2, 4)),
        S((2, 2, 4)),
    ]
    results = pl.pallas_call(
        kernel,
        out_shape=[V(out.shape, out.dtype) for out in outs],
        in_specs=in_specs,
        out_specs=[pl.BlockSpec(memory_space=V)] * 7,
        scratch_shapes=scratch,
        compiler_params=pltpu.CompilerParams(
            collective_id=0, has_side_effects=True, vmem_limit_bytes=56 * 1024 * 1024
        ),
    )(*args)
    return pl.pallas_call(
        hand_on,
        out_shape=outs,
        in_specs=[any_spec] * 7,
        out_specs=[any_spec] * 7,
        scratch_shapes=[S((7,))],
    )(*[pltpu.with_memory_space_constraint(result, V) for result in results])


def solution(mesh):
    return jax.shard_map(
        local,
        mesh=mesh,
        in_specs=(
            P("ctx", "patch"),
            P(None, "patch"),
            P(),
            P(None, "patch"),
            P("ctx", "patch"),
            P("ctx", "patch"),
            P("ctx", "patch"),
            P("ctx", "patch"),
            P("ctx", "patch"),
            P("ctx", "patch"),
            P("ctx", "patch"),
            P(),
        ),
        out_specs=(P("ctx", "patch"),) * 7,
        check_vma=False,
    )
```
